128 devices in a mesh: ctx: 16 (over x_lo, y, core), tp: 8 (over x_hi, z).
Axes of the slice: x: 4 (x_hi: 2, x_lo: 2; x = x_hi * 2 + x_lo), y: 4, z: 4, core: 2. Of those that a mesh axis runs over, the one named last changes fastest.
Arguments:
- activations: bfloat16 [4096, 8192], P('ctx', 'tp'), may hold values from -6 to 6
- proj_weight: bfloat16 [8192, 12288], P('tp'), may hold values from -0.0625 to 0.0625
- filter_taps: float32 [4096, 4096], P(None, ('ctx', 'tp')), may hold values from -0.09375 to 0.09375
- filter_blocks: int32 [4096], replicated, may hold values from 1 to 16, as said below
- skip_gain: float32 [4096], replicated, may hold values from 0.5 to 1.5
Outputs:
- mixed_out: bfloat16 [4096, 4096], P(None, ('ctx', 'tp'))
The draws below stay inside these ranges and needn't reach their ends.
Inputs may be any that keep to these rules, and one draw needn't show every extreme that they name: `filter_blocks`: some channel has exactly 1 block and some channel has all 16 blocks.
All inputs are finite; a program needn't handle non-finite values.
Results may differ from the reference program's by a relative error of at most 0.025.
Values may be sent and summed in bfloat16 or wider, within the bound.
A program may use at most 128 MiB of HBM per device.

```python
import jax
import jax.numpy as jnp
from jax import lax

D = 8192
C = 4096
TOK_DEV = 256
TOKENS = 4096
N_TP = 8


def draw_filter_blocks(key, part):
    key = jax.random.fold_in(key, 7)
    first_key, second_key = jax.random.split(key)
    count = TOKENS // TOK_DEV
    blocks = jax.random.randint(first_key, (C,), 1, count + 1)
    order = jax.random.permutation(second_key, C)
    blocks = blocks.at[order[0]].set(count)
    blocks = blocks.at[order[1]].set(1)
    return blocks.astype(jnp.int32)


def shard_levels(own_key, shape, pieces, least, top_value):
    factor_of, own = 1.0, jax.random.fold_in(own_key, 6)
    for axis_at, shards_of in pieces:
        steps = jnp.exp(jax.random.uniform(jax.random.fold_in(own, axis_at), (shards_of,), jnp.float32, least / len(pieces), top_value / len(pieces)))
        factor_of = factor_of * jnp.repeat(steps, shape[axis_at] // shards_of).reshape([-1 if axis == axis_at else 1 for axis in range(len(shape))])
    return factor_of


def noise(own_key, shape, deviation, bound, cuts=(), kind=jnp.bfloat16):
    values = jax.random.normal(own_key, shape, jnp.float32) * deviation
    if len(cuts) > 0:
        values = shard_levels(own_key, shape, cuts, -0.22, 0.18) * values
    return jnp.clip(values, min=-bound, max=bound).astype(kind)


def setup_inputs(seed: int = 0) -> dict:
    splits = jax.random.split(jax.random.key(seed), 6)
    activations = noise(splits[0], (TOKENS, D), 1.0, 6.0, ((0, 16), (1, 8)))
    proj_weight = noise(splits[1], (D, 3 * C), D ** -0.5, 0.0625, ((0, 8),))
    filter_taps = noise(splits[2], (C, TOKENS), TOKENS ** -0.5, 0.09375, ((1, 128),), jnp.float32)
    filter_blocks = draw_filter_blocks(jax.random.fold_in(splits[5], 71), 0)
    skip_gain = jnp.clip(jax.random.uniform(splits[4], (C,), jnp.float32, 0.5, 1.5), 0.5, 1.5)
    return dict(activations=activations, proj_weight=proj_weight, filter_taps=filter_taps, filter_blocks=filter_blocks, skip_gain=skip_gain)


def reference(activations, proj_weight, filter_taps, filter_blocks, skip_gain):
    tokens, width = activations.shape
    channels = filter_taps.shape[0]
    rows_each = width // N_TP
    projected = jnp.zeros((tokens, 3 * channels), jnp.float32)
    for group in range(N_TP):
        block = jnp.dot(activations[:, group * rows_each:(group + 1) * rows_each],
                        proj_weight[group * rows_each:(group + 1) * rows_each],
                        preferred_element_type=jnp.float32)
        rounded = lax.optimization_barrier(block.astype(jnp.bfloat16))
        projected = projected + rounded.astype(jnp.float32)
    query_rows = projected[:, :channels].T
    key_rows = projected[:, channels:2 * channels].T
    value_rows = projected[:, 2 * channels:].T
    gated = key_rows * value_rows
    positions = jnp.arange(tokens, dtype=jnp.int32)
    live_mask = positions[None, :] < filter_blocks[:, None] * TOK_DEV
    kept = jnp.where(live_mask, filter_taps, jnp.zeros_like(filter_taps))
    spectrum = jnp.fft.rfft(gated, n=2 * tokens, axis=1) * jnp.fft.rfft(kept, n=2 * tokens, axis=1)
    convolved = jnp.fft.irfft(spectrum, n=2 * tokens, axis=1)[:, :tokens]
    result = query_rows * (convolved + skip_gain[:, None] * gated)
    return result.astype(jnp.bfloat16)
```

```python
import functools
import math

import jax
import jax.numpy as jnp
import ml_dtypes
import numpy as np
from jax import lax
from jax.experimental import pallas as pl
from jax.experimental.pallas import tpu as pltpu
from jax.sharding import PartitionSpec as P

BF = jnp.bfloat16
F32 = jnp.float32
OUTER = 32
INNER = 128
LENGTH = OUTER * INNER
SHIFT = 0.25

ROWS_Z = 144
LANES_Z = 2304


def flipped(index):
    return int(format(index, "05b")[::-1], 2)


def tables():
    at = np.arange(INNER)
    angle = 2.0 * math.pi * (at[:, None] * at[None, :] % INNER) / INNER
    cos, sin = np.cos(angle), np.sin(angle)
    forward = np.block([[cos, -sin], [sin, cos]])
    inverse = np.block([[cos, sin], [-sin, cos]])
    freqs = np.array([flipped(f) for f in range(OUTER)]) + SHIFT
    turn = 2.0 * math.pi * freqs[:, None] * at[None, :] / LENGTH

    def halves(matrix):
        high = matrix.astype(ml_dtypes.bfloat16)
        low = (matrix - high.astype(np.float64)).astype(ml_dtypes.bfloat16)
        return np.stack([high, low])

    twiddle = np.stack([np.cos(turn), np.sin(turn)]).astype(np.float32)
    return halves(forward), halves(inverse / LENGTH), twiddle


def times(pair, turn):
    re, im = pair
    turn = turn % 1.0
    if turn == 0.0:
        return pair
    if turn == 0.25:
        return (-im, re)
    if turn == 0.5:
        return (-re, -im)
    if turn == 0.75:
        return (im, -re)
    c, s = math.cos(2 * math.pi * turn), math.sin(2 * math.pi * turn)
    return (re * c - im * s, re * s + im * c)


def outer_forward(blocks):
    data = []
    for a, block in enumerate(blocks):
        angle = -2.0 * math.pi * a * SHIFT / OUTER
        data.append((block * math.cos(angle), block * math.sin(angle)) if a else (block, jnp.zeros_like(block)))
    half = OUTER // 2
    while half >= 1:
        for start in range(0, OUTER, 2 * half):
            for k in range(half):
                a, b = data[start + k], data[start + k + half]
                data[start + k] = (a[0] + b[0], a[1] + b[1])
                data[start + k + half] = times((a[0] - b[0], a[1] - b[1]), -k / (2 * half))
        half //= 2
    return data


def outer_inverse(data):
    data = list(data)
    half = 1
    while half < OUTER:
        for start in range(0, OUTER, 2 * half):
            for k in range(half):
                a, b = data[start + k], times(data[start + k + half], k / (2 * half))
                data[start + k] = (a[0] + b[0], a[1] + b[1])
                data[start + k + half] = (a[0] - b[0], a[1] - b[1])
        half *= 2
    out = []
    for a, (re, im) in enumerate(data):
        angle = 2.0 * math.pi * a * SHIFT / OUTER
        out.append(re * math.cos(angle) - im * math.sin(angle))
    return out


class Spread:
    def __init__(self, place, links, part, bufs):
        self.place, self.links, self.part = place, links, part
        self.z1, self.z2, self.zx, self.x1, self.x2, self.x3 = bufs
        self.pending = {}

    def cell(self, own, step, piece, half):
        return self.part(self.place.owner(own, step), piece, half)

    def send(self, key, src, dst, to):
        self.pending[key] = self.links.send(src, dst, to)

    def start_z1(self, own):
        for way in (0, 1):
            self.send(("z1", own, way), self.cell(own, 2, 0, way), self.z1.at[way, own], self.place.zway[way])

    def start_x1(self, step):
        for half in (0, 1):
            self.send(("x1", step, half), self.cell(0, step, 1, half), self.x1.at[step, half], self.place.far)

    def start_z2_free(self, own, way):
        step = (1, 3)[way]
        self.send(("z2", own, way, 1 - way), self.cell(own, step, 0, 1 - way), self.z2.at[way, own, 1 - way], self.place.zway[way])

    def pass_z1(self, own, way):
        self.pending[("z1", own, way)].wait_recv()
        cell = self.cell(own, (1, 3)[way], 0, way)
        cell[...] = (cell[...].astype(F32) + self.z1[way, own].astype(F32)).astype(BF)
        self.send(("z2", own, way, way), cell, self.z2.at[way, own, way], self.place.zway[way])

    def take_x1(self, step):
        for half in (0, 1):
            self.pending[("x1", step, half)].wait_recv()
            cell = self.cell(1, step, 1, half)
            cell[...] = (cell[...].astype(F32) + self.x1[step, half].astype(F32)).astype(BF)

    def start_x2(self):
        for way in (0, 1):
            self.send(("x2", way), self.cell(1, 2, 1, way), self.x2.at[way], self.place.zway[way])

    def start_x3_free(self, way):
        self.send(("x3", way, 1 - way), self.cell(1, (1, 3)[way], 1, 1 - way), self.x3.at[way, 1 - way], self.place.zway[way])

    def pass_x2(self, way):
        self.pending[("x2", way)].wait_recv()
        cell = self.cell(1, (1, 3)[way], 1, way)
        cell[...] = (cell[...].astype(F32) + self.x2[way].astype(F32)).astype(BF)
        self.send(("x3", way, way), cell, self.x3.at[way, way], self.place.zway[way])

    def wait_z2(self, own):
        for way in (0, 1):
            for half in (0, 1):
                self.pending[("z2", own, way, half)].wait_recv()

    def start_zx(self):
        self.wait_z2(0)
        for half in (0, 1):
            cell = self.cell(0, 0, 0, half)
            total = cell[...].astype(F32) + self.z2[0, 0, half].astype(F32) + self.z2[1, 0, half].astype(F32)
            cell[...] = total.astype(BF)
            self.send(("zx", half), cell, self.zx.at[half], self.place.far)

    def finish(self):
        self.wait_z2(1)
        for half in (0, 1):
            self.pending[("x1", 0, half)].wait_recv()
            for way in (0, 1):
                self.pending[("x3", way, half)].wait_recv()
        for half in (0, 1):
            self.pending[("zx", half)].wait_recv()

    def total(self, piece, half):
        mine = self.cell(1, 0, piece, half)[...].astype(F32)
        if piece == 0:
            terms = (self.z2[0, 1, half], self.z2[1, 1, half], self.zx[half])
        else:
            terms = (self.x1[0, half], self.x3[0, half], self.x3[1, half])
        for term in terms:
            mine = mine + term.astype(F32)
        return mine


class Place:
    def __init__(self, depth, tp_count, ctx_count):
        self.ctx, self.tp = lax.axis_index("ctx"), lax.axis_index("tp")
        self.depth, self.tp_count, self.ctx_count = depth, tp_count, ctx_count
        self.x_half, self.z = self.tp // depth, self.tp % depth
        self.zway = tuple((self.ctx, self.x_half * depth + (self.z + step) % depth) for step in (1, depth - 1))
        self.far = (self.ctx, (self.tp + depth) % tp_count)

    def owner(self, own, step):
        half = self.x_half if own else 1 - self.x_half
        return half * self.depth + (self.z + step) % self.depth


class Links:
    def __init__(self, send_sems, recv_sems):
        self.send_sems, self.recv_sems = send_sems, recv_sems
        self.used = 0
        self.started = []

    def make(self, src, dst, to, at):
        return pltpu.make_async_remote_copy(
            src_ref=src,
            dst_ref=dst,
            send_sem=self.send_sems.at[at],
            recv_sem=self.recv_sems.at[at],
            device_id=to,
            device_id_type=pl.DeviceIdType.MESH,
        )

    def send(self, src, dst, to):
        copy = self.make(src, dst, to, self.used)
        self.used += 1
        copy.start()
        self.started.append(copy)
        return copy


class Swap:
    def __init__(self, links, count, me, device, src, dst):
        self.links, self.count, self.me, self.device, self.src, self.dst = links, count, me, device, src, dst
        self.base = links.used
        links.used += count - 1

    def copy(self, away):
        peer = (self.me + away) % self.count
        return self.links.make(self.src(peer), self.dst(self.me), self.device(peer), self.base + away - 1)

    def each(self, act):
        lax.fori_loop(1, self.count, lambda away, carry: (act(self.copy(away)), carry)[1], 0)

    def start(self):
        self.each(lambda copy: copy.start())

    def wait_recv(self):
        self.each(lambda copy: copy.wait_recv())

    def wait_send(self):
        self.each(lambda copy: copy.wait_send())


def transposed(source, target, rows, lanes):
    for r in range(0, rows, 128):
        for c in range(0, lanes, 128):
            tile = source[pl.ds(r, 128), pl.ds(c, 128)].astype(F32)
            target[pl.ds(c, 128), pl.ds(r, 128)] = tile.T.astype(target.dtype)


def spectrum(source, staged, twiddle):
    ctx_count, lanes, span = source.shape
    fold = span // INNER

    def group(g, carry):
        at = pl.multiple_of(g * 16, 16)
        blocks = []
        for i in range(ctx_count):
            for u in range(fold):
                blocks.append(source[i, pl.ds(at, 16), pl.ds(u * INNER, INNER)].astype(F32))
        for f, (re, im) in enumerate(outer_forward(blocks)):
            c, s = twiddle[0, pl.ds(f, 1), :], twiddle[1, pl.ds(f, 1), :]
            row = pl.ds(pl.multiple_of(f * lanes + at, 16), 16)
            staged[row, pl.ds(0, INNER)] = (re * c + im * s).astype(BF)
            staged[row, pl.ds(INNER, INNER)] = (im * c - re * s).astype(BF)
        return carry

    lax.fori_loop(0, lanes // 16, group, 0)


def both(data, matrix):
    return jnp.dot(data, matrix[0], preferred_element_type=F32) + jnp.dot(data, matrix[1], preferred_element_type=F32)


def kernel(
    act, weight, taps, blocks, gains, forward, inverse, twiddle,
    out,
    wbuf, kv, qs,
    kv_z1, kv_z2, kv_zx, kv_x1, kv_x2, kv_x3,
    q_z1, q_z2, q_zx, q_x1, q_x2, q_x3,
    taps_in, taps_t, filt_in, staged, filt_spec,
    gated, gated_t, gated_in, mixed, conv_out, conv_in, conv_t, conv_home, conv_final,
    w_sems, send_sems, recv_sems,
    *, depth, tp_count, ctx_count,
):
    place = Place(depth, tp_count, ctx_count)
    me, tp = place.ctx, place.tp
    tokens, width = gated.shape
    lanes = width // ctx_count
    out_tokens = tokens // tp_count
    channels = tp_count * width
    tile = wbuf.shape[2]

    order = [(0, 2), (1, 2), (0, 1), (0, 3), (1, 1), (1, 3), (0, 0), (1, 0)]
    columns = []
    for own, step in order:
        for which in (1, 2):
            columns.append(which * channels + place.owner(own, step) * width)
    for t in range(channels // tile):
        columns.append(t * tile)

    def fetch(t):
        return pltpu.make_async_copy(weight.at[:, pl.ds(pl.multiple_of(columns[t], tile), tile)], wbuf.at[t], w_sems.at[t])

    ahead = 8
    for t in range(ahead):
        fetch(t).start()

    barrier = pltpu.get_barrier_semaphore()

    def greet(device, count, mine):
        def body(away, carry):
            pl.semaphore_signal(barrier, inc=1, device_id=device((mine + away) % count), device_id_type=pl.DeviceIdType.MESH)
            return carry
        lax.fori_loop(1, count, body, 0)

    greet(lambda peer: (me, peer), tp_count, tp)
    greet(lambda peer: (peer, tp), ctx_count, me)
    pl.semaphore_wait(barrier, tp_count + ctx_count - 2)

    links = Links(send_sems, recv_sems)

    def over_tp(src, dst):
        return Swap(links, tp_count, tp, lambda peer: (me, peer), src, dst)

    def over_ctx(src, dst):
        return Swap(links, ctx_count, me, lambda peer: (peer, tp), src, dst)

    def wide(ref, index, size):
        return ref.at[pl.ds(pl.multiple_of(index * size, size), size)]

    tap_swap = over_tp(lambda peer: taps.at[:, pl.ds(pl.multiple_of(peer * width, width), width)], lambda mine: wide(taps_in, mine, out_tokens))
    filt_swap = over_ctx(lambda peer: wide(taps_t, peer, lanes), lambda mine: filt_in.at[mine])
    gated_swap = over_ctx(lambda peer: wide(gated_t, peer, lanes), lambda mine: gated_in.at[mine])
    conv_swap = over_ctx(lambda peer: conv_out.at[peer], lambda mine: wide(conv_in, mine, lanes))
    home_swap = over_tp(lambda peer: wide(conv_home, peer, out_tokens), lambda mine: conv_final.at[mine])

    def kv_part(owner, piece, half):
        rows = pl.ds(0, ROWS_Z) if piece == 0 else pl.ds(ROWS_Z, tokens - ROWS_Z)
        return kv.at[owner, rows, pl.ds(half * width, width)]

    z_half, x_half = LANES_Z // 2, (channels - LANES_Z) // 2

    def q_part(owner, piece, half):
        return qs.at[owner, :, pl.ds(half * z_half, z_half) if piece == 0 else pl.ds(LANES_Z + half * x_half, x_half)]

    first = Spread(place, links, kv_part, (kv_z1, kv_z2, kv_zx, kv_x1, kv_x2, kv_x3))
    second = Spread(place, links, q_part, (q_z1, q_z2, q_zx, q_x1, q_x2, q_x3))

    tap_swap.start()

    sub = 256
    for n, (own, step) in enumerate(order):
        owner = place.owner(own, step)
        for which in (0, 1):
            t = 2 * n + which
            fetch(t).wait()
            if t + ahead < len(columns):
                fetch(t + ahead).start()

            def multiply(s, carry):
                at = pl.ds(pl.multiple_of(s * sub, sub), sub)
                to = pl.ds(pl.multiple_of(which * width + s * sub, sub), sub)
                kv[owner, :, to] = jnp.dot(act[...], wbuf[t, :, at], preferred_element_type=F32).astype(BF)
                return carry

            lax.fori_loop(0, width // sub, multiply, 0)
        if step == 2:
            first.start_z1(own)
        elif step == 1:
            first.start_z2_free(own, 0)
        elif step == 3:
            first.start_z2_free(own, 1)
        if own == 0:
            first.start_x1(step)

    tap_swap.wait_recv()
    wide(taps_in, tp, out_tokens)[...] = taps[:, pl.ds(pl.multiple_of(tp * width, width), width)]
    live = me < blocks[pl.ds(tp, 1), :]
    for r in range(0, tokens, 128):
        for c in range(0, width, 128):
            block = taps_in[pl.ds(r, 128), pl.ds(c, 128)].astype(F32)
            block = jnp.where(live[:, c:c + 128], block, 0.0)
            taps_t[pl.ds(c, 128), pl.ds(r, 128)] = block.T.astype(BF)
    filt_swap.start()

    for own in (0, 1):
        for way in (0, 1):
            first.pass_z1(own, way)

    for t in range(2 * len(order), len(columns)):
        fetch(t).wait()
        if t + ahead < len(columns):
            fetch(t + ahead).start()

        def multiply(s, carry):
            at = pl.ds(pl.multiple_of(s * sub, sub), sub)
            to = pl.ds(pl.multiple_of((t - 2 * len(order)) * tile + s * sub, sub), sub)
            block = jnp.dot(act[...], wbuf[t, :, at], preferred_element_type=F32).astype(BF)
            qs[:, :, to] = block.reshape(tp_count, out_tokens, sub)
            return carry

        lax.fori_loop(0, tile // sub, multiply, 0)

    first.take_x1(2)
    first.start_x2()
    first.take_x1(1)
    first.start_x3_free(0)
    first.take_x1(3)
    first.start_x3_free(1)

    filt_swap.wait_recv()
    filt_in[me] = wide(taps_t, me, lanes)[...]
    spectrum(filt_in, staged, twiddle)
    rows = staged.shape[0] // 4

    def filter_tile(n, carry):
        at = pl.ds(pl.multiple_of(n * rows, rows), rows)
        filt_spec[at, :] = both(staged[at, :], forward)
        return carry

    lax.fori_loop(0, 4, filter_tile, 0)

    first.start_zx()
    for way in (0, 1):
        first.pass_x2(way)

    for own in (0, 1):
        second.start_z1(own)
    for step in (2, 1, 3, 0):
        second.start_x1(step)
    for own in (0, 1):
        for way in (0, 1):
            second.start_z2_free(own, way)

    first.finish()
    for piece, at in ((0, pl.ds(0, ROWS_Z)), (1, pl.ds(ROWS_Z, tokens - ROWS_Z))):
        gated[at, :] = first.total(piece, 0) * first.total(piece, 1)
    transposed(gated, gated_t, tokens, width)
    gated_swap.start()

    for own in (0, 1):
        for way in (0, 1):
            second.pass_z1(own, way)
    second.take_x1(2)
    second.start_x2()
    second.take_x1(1)
    second.start_x3_free(0)
    second.take_x1(3)
    second.start_x3_free(1)

    gated_swap.wait_recv()
    gated_in[me] = wide(gated_t, me, lanes)[...]
    spectrum(gated_in, staged, twiddle)
    per = rows // lanes

    def mix_tile(n, carry):
        at = pl.ds(pl.multiple_of(n * rows, rows), rows)
        a = both(staged[at, :], forward)
        b = filt_spec[at, :]
        a_re, a_im, b_re, b_im = a[:, :INNER], a[:, INNER:], b[:, :INNER], b[:, INNER:]
        prod = jnp.concatenate([a_re * b_re - a_im * b_im, a_re * b_im + a_im * b_re], axis=1)
        mixed[at, :] = both(prod.astype(BF), inverse)
        return carry

    lax.fori_loop(0, 4, mix_tile, 0)

    def unmix(g, carry):
        at = pl.multiple_of(g * 16, 16)
        data = []
        for f in range(OUTER):
            c, s = twiddle[0, pl.ds(f, 1), :], twiddle[1, pl.ds(f, 1), :]
            row = pl.ds(pl.multiple_of(f * lanes + at, 16), 16)
            re, im = mixed[row, pl.ds(0, INNER)], mixed[row, pl.ds(INNER, INNER)]
            data.append((re * c - im * s, re * s + im * c))
        fold = tokens // INNER
        for a, block in enumerate(outer_inverse(data)):
            conv_out[a // fold, pl.ds(at, 16), pl.ds(a % fold * INNER, INNER)] = block.astype(BF)
        return carry

    lax.fori_loop(0, lanes // 16, unmix, 0)
    conv_swap.start()

    second.start_zx()
    for way in (0, 1):
        second.pass_x2(way)

    conv_swap.wait_recv()
    wide(conv_in, me, lanes)[...] = conv_out[me]
    transposed(conv_in, conv_t, width, tokens)
    conv_home[...] = (conv_t[...] + gains[pl.ds(tp, 1), :] * gated[...]).astype(BF)
    home_swap.start()

    second.finish()
    home_swap.wait_recv()
    conv_final[tp] = wide(conv_home, tp, out_tokens)[...]
    query = jnp.concatenate([second.total(piece, half) for piece in (0, 1) for half in (0, 1)], axis=1)
    for j in range(tp_count):
        at = slice(j * width, (j + 1) * width)
        out[:, at] = (query[:, at] * conv_final[j].astype(F32)).astype(BF)

    for copy in links.started:
        copy.wait_send()
    for swap in (tap_swap, filt_swap, gated_swap, conv_swap, home_swap):
        swap.wait_send()


def on_device(activations, proj_weight, filter_taps, filter_blocks, skip_gain):
    tokens, depth_here = activations.shape
    channels, out_tokens = filter_taps.shape
    tp_count, ctx_count = lax.axis_size("tp"), lax.axis_size("ctx")
    depth = 4
    width = channels // tp_count
    lanes = width // ctx_count
    forward, inverse, twiddle = tables()

    def buffers(z_rows, z_lanes, x_rows, x_lanes):
        return [
            pltpu.VMEM((2, 2, z_rows, z_lanes), BF),
            pltpu.VMEM((2, 2, 2, z_rows, z_lanes), BF),
            pltpu.VMEM((2, z_rows, z_lanes), BF),
            pltpu.VMEM((4, 2, x_rows, x_lanes), BF),
            pltpu.VMEM((2, x_rows, x_lanes), BF),
            pltpu.VMEM((2, 2, x_rows, x_lanes), BF),
        ]

    tile = 512
    n_copies = 2 * 28 + 2 * (tp_count - 1) + 3 * (ctx_count - 1)
    spec_rows = OUTER * lanes
    scratch = (
        [
            pltpu.VMEM((3 * channels // tile, depth_here, tile), BF),
            pltpu.VMEM((tp_count, tokens, 2 * width), BF),
            pltpu.VMEM((tp_count, out_tokens, channels), BF),
        ]
        + buffers(ROWS_Z, width, tokens - ROWS_Z, width)
        + buffers(out_tokens, LANES_Z // 2, out_tokens, (channels - LANES_Z) // 2)
        + [
            pltpu.VMEM((tokens, width), BF),
            pltpu.VMEM((width, tokens), BF),
            pltpu.VMEM((ctx_count, lanes, tokens), BF),
            pltpu.VMEM((spec_rows, 2 * INNER), BF),
            pltpu.VMEM((spec_rows, 2 * INNER), F32),
            pltpu.VMEM((tokens, width), F32),
            pltpu.VMEM((width, tokens), BF),
            pltpu.VMEM((ctx_count, lanes, tokens), BF),
            pltpu.VMEM((spec_rows, 2 * INNER), F32),
            pltpu.VMEM((ctx_count, lanes, tokens), BF),
            pltpu.VMEM((width, tokens), BF),
            pltpu.VMEM((tokens, width), F32),
            pltpu.VMEM((tokens, width), BF),
            pltpu.VMEM((tp_count, out_tokens, width), BF),
            pltpu.SemaphoreType.DMA((3 * channels // tile,)),
            pltpu.SemaphoreType.DMA((n_copies,)),
            pltpu.SemaphoreType.DMA((n_copies,)),
        ]
    )
    vmem = pl.BlockSpec(memory_space=pltpu.VMEM)
    out = pl.pallas_call(
        functools.partial(kernel, depth=depth, tp_count=tp_count, ctx_count=ctx_count),
        out_shape=jax.ShapeDtypeStruct((out_tokens, channels), BF),
        in_specs=[vmem, pl.BlockSpec(memory_space=pl.ANY)] + [vmem] * 6,
        out_specs=vmem,
        scratch_shapes=scratch,
        compiler_params=pltpu.CompilerParams(collective_id=0, has_side_effects=True, vmem_limit_bytes=60 * 2**20),
        name="hyena",
    )(
        activations,
        proj_weight,
        filter_taps.T.astype(BF),
        filter_blocks.reshape(tp_count, width),
        skip_gain.reshape(tp_count, width),
        jnp.asarray(forward),
        jnp.asarray(inverse),
        jnp.asarray(twiddle),
    )
    return out.T


def solution(mesh):
    placed = (P("ctx", "tp"), P("tp", None), P(None, ("ctx", "tp")), P(), P())
    return jax.shard_map(
        on_device, mesh=mesh, in_specs=placed, out_specs=P(None, ("ctx", "tp")), check_vma=False
    )
```

```python
import functools
import math

import jax
import jax.numpy as jnp
import ml_dtypes
import numpy as np
from jax import lax
from jax.experimental import pallas as pl
from jax.experimental.pallas import tpu as pltpu
from jax.sharding import PartitionSpec as P

BF = jnp.bfloat16
F32 = jnp.float32
OUTER = 32
INNER = 128
LENGTH = OUTER * INNER
SETS = 2
SHIFT = 0.25

ROWS_Z = 160
LANES_Z = 2816

SCHEDULE = (
    ("mm", 0, 2), ("mm", 1, 2), ("bar",), ("x1", 0, 2), ("z1", 0, 0), ("tap",), ("z1", 0, 1), ("x1", 1, 2), ("mm", 0, 1),
    ("mm", 0, 3), ("x1", 0, 1), ("z2f", 0, 0, 1), ("mm", 1, 1), ("mm", 1, 3), ("pz1", 0, 0, 0), ("z2f", 0, 1, 1), ("x1", 0, 3),
    ("tx1", 0, 2), ("mm", 0, 0), ("x1", 0, 0), ("x2", 0), ("z2f", 1, 0, 0), ("z2f", 0, 0, 0), ("pz1", 0, 0, 1), ("z1", 1, 0),
    ("x1", 1, 1), ("mm", 1, 0), ("tx1", 1, 2), ("mq", 0), ("mq", 1), ("pz1", 0, 1, 1), ("pz1", 0, 1, 0), ("zx", 0, 0), ("x2", 1),
    ("z2f", 0, 1, 0), ("mask",), ("zx", 0, 1), ("tx1", 0, 3), ("x3f", 0, 1), ("px2", 0, 1), ("tx1", 0, 1), ("x3f", 0, 0),
    ("px2", 0, 0), ("z2f", 1, 0, 1), ("mq", 2), ("pz1", 1, 0, 0), ("pz1", 1, 0, 1), ("x1", 1, 3), ("tx1", 1, 1), ("z1", 1, 1),
    ("x1", 1, 0), ("mq", 3), ("px2", 1, 0), ("z2f", 1, 1, 1), ("x1", 2, 2), ("z2f", 2, 0, 0), ("filt",), ("fin", 0), ("gate", 0),
    ("zx", 1, 1), ("zx", 1, 0), ("pz1", 1, 1, 0), ("pz1", 1, 1, 1), ("tx1", 1, 3), ("x3f", 1, 1), ("x1", 2, 1), ("px2", 1, 1),
    ("z2f", 1, 1, 0), ("x3f", 1, 0), ("z1", 2, 0), ("z2f", 2, 0, 1), ("x1", 2, 3), ("tx1", 2, 2), ("z2f", 2, 1, 0), ("conv", 0),
    ("fin", 1), ("gate", 1), ("pz1", 2, 0, 1), ("pz1", 2, 0, 0), ("tx1", 2, 1), ("x3f", 2, 0), ("x2", 2), ("tx1", 2, 3),
    ("x3f", 2, 1), ("x1", 2, 0), ("z2f", 2, 1, 1), ("z1", 2, 1), ("home", 0), ("conv", 1), ("px2", 2, 0), ("px2", 2, 1),
    ("zx", 2, 1), ("zx", 2, 0), ("pz1", 2, 1, 0), ("pz1", 2, 1, 1), ("home", 1), ("fin", 2), ("out",),
)


def flipped(index):
    return int(format(index, "05b")[::-1], 2)


def tables():
    at = np.arange(INNER)
    angle = 2.0 * math.pi * (at[:, None] * at[None, :] % INNER) / INNER
    cos, sin = np.cos(angle), np.sin(angle)
    forward = np.block([[cos, -sin], [sin, cos]])
    inverse = np.block([[cos, sin], [-sin, cos]])
    freqs = np.array([flipped(f) for f in range(OUTER)]) + SHIFT
    turn = 2.0 * math.pi * freqs[:, None] * at[None, :] / LENGTH

    def halves(matrix):
        high = matrix.astype(ml_dtypes.bfloat16)
        low = (matrix - high.astype(np.float64)).astype(ml_dtypes.bfloat16)
        return np.stack([high, low])

    twiddle = np.stack([np.cos(turn), np.sin(turn)]).astype(np.float32)
    return halves(forward), halves(inverse / LENGTH), twiddle


def times(pair, turn):
    re, im = pair
    turn = turn % 1.0
    if turn == 0.0:
        return pair
    if turn == 0.25:
        return (-im, re)
    if turn == 0.5:
        return (-re, -im)
    if turn == 0.75:
        return (im, -re)
    c, s = math.cos(2 * math.pi * turn), math.sin(2 * math.pi * turn)
    return (re * c - im * s, re * s + im * c)


def outer_forward(blocks):
    data = []
    for a, block in enumerate(blocks):
        angle = -2.0 * math.pi * a * SHIFT / OUTER
        data.append((block * math.cos(angle), block * math.sin(angle)) if a else (block, jnp.zeros_like(block)))
    half = OUTER // 2
    while half >= 1:
        for start in range(0, OUTER, 2 * half):
            for k in range(half):
                a, b = data[start + k], data[start + k + half]
                data[start + k] = (a[0] + b[0], a[1] + b[1])
                data[start + k + half] = times((a[0] - b[0], a[1] - b[1]), -k / (2 * half))
        half //= 2
    return data


def outer_inverse(data):
    data = list(data)
    half = 1
    while half < OUTER:
        for start in range(0, OUTER, 2 * half):
            for k in range(half):
                a, b = data[start + k], times(data[start + k + half], k / (2 * half))
                data[start + k] = (a[0] + b[0], a[1] + b[1])
                data[start + k + half] = (a[0] - b[0], a[1] - b[1])
        half *= 2
    out = []
    for a, (re, im) in enumerate(data):
        angle = 2.0 * math.pi * a * SHIFT / OUTER
        out.append(re * math.cos(angle) - im * math.sin(angle))
    return out


class Spread:
    def __init__(self, place, links, part, bufs):
        self.place, self.links, self.part = place, links, part
        self.z1, self.z2, self.zx, self.x1, self.x2, self.x3 = bufs
        self.pending = {}

    def cell(self, own, step, piece, half):
        return self.part(self.place.owner(own, step), piece, half)

    def send(self, key, src, dst, to):
        self.pending[key] = self.links.send(src, dst, to)

    def start_z1(self, own):
        for way in (0, 1):
            self.send(("z1", own, way), self.cell(own, 2, 0, way), self.z1.at[way, own], self.place.zway[way])

    def start_x1(self, step):
        for half in (0, 1):
            self.send(("x1", step, half), self.cell(0, step, 1, half), self.x1.at[step, half], self.place.far)

    def start_z2_free(self, own, way):
        step = (1, 3)[way]
        self.send(("z2", own, way, 1 - way), self.cell(own, step, 0, 1 - way), self.z2.at[way, own, 1 - way], self.place.zway[way])

    def pass_z1(self, own, way):
        self.pending[("z1", own, way)].wait_recv()
        cell = self.cell(own, (1, 3)[way], 0, way)
        cell[...] = (cell[...].astype(F32) + self.z1[way, own].astype(F32)).astype(BF)
        self.send(("z2", own, way, way), cell, self.z2.at[way, own, way], self.place.zway[way])

    def take_x1(self, step):
        for half in (0, 1):
            self.pending[("x1", step, half)].wait_recv()
            cell = self.cell(1, step, 1, half)
            cell[...] = (cell[...].astype(F32) + self.x1[step, half].astype(F32)).astype(BF)

    def start_x2(self):
        for way in (0, 1):
            self.send(("x2", way), self.cell(1, 2, 1, way), self.x2.at[way], self.place.zway[way])

    def start_x3_free(self, way):
        self.send(("x3", way, 1 - way), self.cell(1, (1, 3)[way], 1, 1 - way), self.x3.at[way, 1 - way], self.place.zway[way])

    def pass_x2(self, way):
        self.pending[("x2", way)].wait_recv()
        cell = self.cell(1, (1, 3)[way], 1, way)
        cell[...] = (cell[...].astype(F32) + self.x2[way].astype(F32)).astype(BF)
        self.send(("x3", way, way), cell, self.x3.at[way, way], self.place.zway[way])

    def start_zx(self, half):
        for way in (0, 1):
            self.pending[("z2", 0, way, half)].wait_recv()
        cell = self.cell(0, 0, 0, half)
        total = cell[...].astype(F32) + self.z2[0, 0, half].astype(F32) + self.z2[1, 0, half].astype(F32)
        cell[...] = total.astype(BF)
        self.send(("zx", half), cell, self.zx.at[half], self.place.far)

    def finish(self):
        for half in (0, 1):
            self.pending[("x1", 0, half)].wait_recv()
            for way in (0, 1):
                self.pending[("z2", 1, way, half)].wait_recv()
                self.pending[("x3", way, half)].wait_recv()
            self.pending[("zx", half)].wait_recv()

    def total(self, piece, half):
        mine = self.cell(1, 0, piece, half)[...].astype(F32)
        if piece == 0:
            terms = (self.z2[0, 1, half], self.z2[1, 1, half], self.zx[half])
        else:
            terms = (self.x1[0, half], self.x3[0, half], self.x3[1, half])
        for term in terms:
            mine = mine + term.astype(F32)
        return mine


class Place:
    def __init__(self, depth, tp_count, ctx_count):
        self.ctx, self.tp = lax.axis_index("ctx"), lax.axis_index("tp")
        self.depth, self.tp_count, self.ctx_count = depth, tp_count, ctx_count
        self.x_half, self.z = self.tp // depth, self.tp % depth
        self.zway = tuple((self.ctx, self.x_half * depth + (self.z + step) % depth) for step in (1, depth - 1))
        self.far = (self.ctx, (self.tp + depth) % tp_count)

    def owner(self, own, step):
        half = self.x_half if own else 1 - self.x_half
        return half * self.depth + (self.z + step) % self.depth


class Links:
    def __init__(self, send_sems, recv_sems):
        self.send_sems, self.recv_sems = send_sems, recv_sems
        self.used = 0
        self.started = []

    def make(self, src, dst, to, at):
        return pltpu.make_async_remote_copy(
            src_ref=src,
            dst_ref=dst,
            send_sem=self.send_sems.at[at],
            recv_sem=self.recv_sems.at[at],
            device_id=to,
            device_id_type=pl.DeviceIdType.MESH,
        )

    def send(self, src, dst, to):
        copy = self.make(src, dst, to, self.used)
        self.used += 1
        copy.start()
        self.started.append(copy)
        return copy


class Swap:
    def __init__(self, links, count, me, device, src, dst):
        self.links, self.count, self.me, self.device, self.src, self.dst = links, count, me, device, src, dst
        self.base = links.used
        links.used += count - 1

    def copy(self, away):
        peer = (self.me + away) % self.count
        return self.links.make(self.src(peer), self.dst(self.me), self.device(peer), self.base + away - 1)

    def each(self, act):
        lax.fori_loop(1, self.count, lambda away, carry: (act(self.copy(away)), carry)[1], 0)

    def start(self):
        self.each(lambda copy: copy.start())

    def wait_recv(self):
        self.each(lambda copy: copy.wait_recv())

    def wait_send(self):
        self.each(lambda copy: copy.wait_send())


def transposed(source, target, rows, lanes):
    for r in range(0, rows, 128):
        for c in range(0, lanes, 128):
            tile = source[pl.ds(r, 128), pl.ds(c, 128)].astype(F32)
            target[pl.ds(c, 128), pl.ds(r, 128)] = tile.T.astype(target.dtype)


def spectrum(source, staged, twiddle):
    ctx_count, lanes, span = source.shape
    blocks = []
    for i in range(ctx_count):
        for u in range(span // INNER):
            blocks.append(source[i, :, pl.ds(u * INNER, INNER)].astype(F32))
    for f, (re, im) in enumerate(outer_forward(blocks)):
        c, s = twiddle[0, pl.ds(f, 1), :], twiddle[1, pl.ds(f, 1), :]
        staged[pl.ds(f * lanes, lanes), pl.ds(0, INNER)] = (re * c + im * s).astype(BF)
        staged[pl.ds(f * lanes, lanes), pl.ds(INNER, INNER)] = (im * c - re * s).astype(BF)


def both(data, matrix):
    return jnp.dot(data, matrix[0], preferred_element_type=F32) + jnp.dot(data, matrix[1], preferred_element_type=F32)


def kernel(
    act, weight, taps, blocks, gains, forward, inverse, twiddle,
    out,
    wbuf, kv, qs,
    a_z1, a_z2, a_zx, a_x1, a_x2, a_x3,
    b_z1, b_z2, b_zx, b_x1, b_x2, b_x3,
    q_z1, q_z2, q_zx, q_x1, q_x2, q_x3,
    taps_out, taps_in, taps_t, filt_in, staged, filt_spec,
    gated, gated_t, gated_in, mixed, conv_out, conv_in, conv_home, conv_final,
    w_sems, send_sems, recv_sems,
    *, depth, tp_count, ctx_count,
):
    place = Place(depth, tp_count, ctx_count)
    me, tp = place.ctx, place.tp
    tokens, width = gated.shape
    out_tokens = tokens // tp_count
    channels = tp_count * width
    tile = wbuf.shape[2]
    piece = width // SETS
    lanes = piece // ctx_count

    order = [step[1:] for step in SCHEDULE if step[0] == "mm"]
    tiles = []
    for own, step in order:
        base = place.owner(own, step) * width
        tiles.append([(which * channels + base + c * piece, piece) for c in range(SETS) for which in (1, 2)])
    for t in range(channels // tile):
        tiles.append([(t * tile, tile)])

    def fetch(t, act_on):
        at = 0
        for k, (column, size) in enumerate(tiles[t]):
            src = weight.at[:, pl.ds(pl.multiple_of(column, size), size)]
            act_on(pltpu.make_async_copy(src, wbuf.at[t, :, pl.ds(at, size)], w_sems.at[4 * t + k]))
            at += size

    ahead = 4
    for t in range(ahead):
        fetch(t, lambda copy: copy.start())

    def next_tile(t):
        fetch(t, lambda copy: copy.wait())
        if t + ahead < len(tiles):
            fetch(t + ahead, lambda copy: copy.start())

    barrier = pltpu.get_barrier_semaphore()

    def greet(device, count, mine):
        def body(away, carry):
            pl.semaphore_signal(barrier, inc=1, device_id=device((mine + away) % count), device_id_type=pl.DeviceIdType.MESH)
            return carry
        lax.fori_loop(1, count, body, 0)

    greet(lambda peer: (me, peer), tp_count, tp)
    greet(lambda peer: (peer, tp), ctx_count, me)

    taps_out[...] = taps[...].astype(BF)

    links = Links(send_sems, recv_sems)

    def over_tp(src, dst):
        return Swap(links, tp_count, tp, lambda peer: (me, peer), src, dst)

    def over_ctx(src, dst):
        return Swap(links, ctx_count, me, lambda peer: (peer, tp), src, dst)

    def span(index, size):
        return pl.ds(pl.multiple_of(index * size, size), size)

    tap_swap = over_tp(lambda peer: taps_out.at[:, span(peer, width)], lambda mine: taps_in.at[span(mine, out_tokens)])
    filt_swap = over_ctx(lambda peer: taps_t.at[:, span(peer, lanes)], lambda mine: filt_in.at[mine])
    gated_swap = [over_ctx(lambda peer, c=c: gated_t.at[c, span(peer, lanes)], lambda mine, c=c: gated_in.at[c, mine]) for c in range(SETS)]
    conv_swap = [over_ctx(lambda peer, c=c: conv_out.at[c, peer], lambda mine, c=c: conv_in.at[c, span(mine, lanes)]) for c in range(SETS)]
    home_swap = [over_tp(lambda peer, c=c: conv_home.at[c, span(peer, out_tokens)], lambda mine, c=c: conv_final.at[c, mine]) for c in range(SETS)]

    def kv_part(c):
        def part(owner, which, half):
            rows = pl.ds(0, ROWS_Z) if which == 0 else pl.ds(ROWS_Z, tokens - ROWS_Z)
            return kv.at[owner, rows, pl.ds((2 * c + half) * piece, piece)]
        return part

    z_half, x_half = LANES_Z // 2, (channels - LANES_Z) // 2

    def q_part(owner, which, half):
        return qs.at[owner, :, pl.ds(half * z_half, z_half) if which == 0 else pl.ds(LANES_Z + half * x_half, x_half)]

    spreads = (
        Spread(place, links, kv_part(0), (a_z1, a_z2, a_zx, a_x1, a_x2, a_x3)),
        Spread(place, links, kv_part(1), (b_z1, b_z2, b_zx, b_x1, b_x2, b_x3)),
        Spread(place, links, q_part, (q_z1, q_z2, q_zx, q_x1, q_x2, q_x3)),
    )

    def multiply_kv(own, step):
        t = order.index((own, step))
        next_tile(t)
        kv[place.owner(own, step)] = jnp.dot(act[...], wbuf[t], preferred_element_type=F32).astype(BF)

    def multiply_q(t):
        next_tile(len(order) + t)
        block = jnp.dot(act[...], wbuf[len(order) + t], preferred_element_type=F32).astype(BF)
        qs[:, :, pl.ds(t * tile, tile)] = block.reshape(tp_count, out_tokens, tile)

    def mask():
        tap_swap.wait_recv()
        taps_in[span(tp, out_tokens), :] = taps_out[:, span(tp, width)]
        live = me < blocks[span(tp, width)].reshape(1, width)
        for c in range(SETS):
            for r in range(0, tokens, 128):
                for k in range(0, piece, 128):
                    at = c * piece + k
                    block = taps_in[pl.ds(r, 128), pl.ds(at, 128)].astype(F32)
                    block = jnp.where(live[:, at:at + 128], block, 0.0)
                    taps_t[c, pl.ds(k, 128), pl.ds(r, 128)] = block.T.astype(BF)
        filt_swap.start()

    rows = staged.shape[1] // 2

    def filter_spectrum():
        filt_swap.wait_recv()
        filt_in[me] = taps_t[:, span(me, lanes), :]
        for c in range(SETS):
            spectrum(filt_in.at[:, c], staged.at[c], twiddle)
            for n in range(2):
                at = pl.ds(n * rows, rows)
                filt_spec[c, at, :] = both(staged[c, at, :], forward)

    def finish(c):
        spreads[c].finish()
        if c < SETS:
            for which, at in ((0, pl.ds(0, ROWS_Z)), (1, pl.ds(ROWS_Z, tokens - ROWS_Z))):
                gated[at, pl.ds(c * piece, piece)] = spreads[c].total(which, 0) * spreads[c].total(which, 1)

    def gate(c):
        transposed(gated.at[:, pl.ds(c * piece, piece)], gated_t.at[c], tokens, piece)
        gated_swap[c].start()

    def convolve(c):
        gated_swap[c].wait_recv()
        gated_in[c, me] = gated_t[c, span(me, lanes), :]
        spectrum(gated_in.at[c], staged.at[c], twiddle)
        for n in range(2):
            at = pl.ds(n * rows, rows)
            a, b = both(staged[c, at, :], forward), filt_spec[c, at, :]
            a_re, a_im, b_re, b_im = a[:, :INNER], a[:, INNER:], b[:, :INNER], b[:, INNER:]
            prod = jnp.concatenate([a_re * b_re - a_im * b_im, a_re * b_im + a_im * b_re], axis=1)
            mixed[at, :] = both(prod.astype(BF), inverse)
        data = []
        for f in range(OUTER):
            cos, sin = twiddle[0, pl.ds(f, 1), :], twiddle[1, pl.ds(f, 1), :]
            row = pl.ds(f * lanes, lanes)
            re, im = mixed[row, pl.ds(0, INNER)], mixed[row, pl.ds(INNER, INNER)]
            data.append((re * cos - im * sin, re * sin + im * cos))
        fold = tokens // INNER
        for a, block in enumerate(outer_inverse(data)):
            conv_out[c, a // fold, :, pl.ds(a % fold * INNER, INNER)] = block.astype(BF)
        conv_swap[c].start()

    def home(c):
        conv_swap[c].wait_recv()
        conv_in[c, span(me, lanes), :] = conv_out[c, me]
        gain = gains[span(tp, width)].reshape(1, width)
        for r in range(0, tokens, 128):
            for k in range(0, piece, 128):
                at = c * piece + k
                conv = conv_in[c, pl.ds(k, 128), pl.ds(r, 128)].astype(F32).T
                total = conv + gain[:, at:at + 128] * gated[pl.ds(r, 128), pl.ds(at, 128)]
                conv_home[c, pl.ds(r, 128), pl.ds(k, 128)] = total.astype(BF)
        home_swap[c].start()

    def finale():
        for c in range(SETS):
            home_swap[c].wait_recv()
            conv_final[c, tp] = conv_home[c, span(tp, out_tokens), :]
        query = jnp.concatenate([spreads[SETS].total(which, half) for which in (0, 1) for half in (0, 1)], axis=1)
        for j in range(tp_count):
            for c in range(SETS):
                at = slice(j * width + c * piece, j * width + (c + 1) * piece)
                out[:, at] = (query[:, at] * conv_final[c, j].astype(F32)).astype(BF)

    steps = {
        "bar": lambda: pl.semaphore_wait(barrier, tp_count + ctx_count - 2),
        "mm": multiply_kv,
        "mq": multiply_q,
        "tap": tap_swap.start,
        "mask": mask,
        "filt": filter_spectrum,
        "z1": lambda c, own: spreads[c].start_z1(own),
        "x1": lambda c, step: spreads[c].start_x1(step),
        "z2f": lambda c, own, way: spreads[c].start_z2_free(own, way),
        "pz1": lambda c, own, way: spreads[c].pass_z1(own, way),
        "tx1": lambda c, step: spreads[c].take_x1(step),
        "x2": lambda c: spreads[c].start_x2(),
        "x3f": lambda c, way: spreads[c].start_x3_free(way),
        "px2": lambda c, way: spreads[c].pass_x2(way),
        "zx": lambda c, half: spreads[c].start_zx(half),
        "fin": finish,
        "gate": gate,
        "conv": convolve,
        "home": home,
        "out": finale,
    }
    for step in SCHEDULE:
        steps[step[0]](*step[1:])

    for copy in links.started:
        copy.wait_send()
    for swap in [tap_swap, filt_swap] + gated_swap + conv_swap + home_swap:
        swap.wait_send()


def on_device(activations, proj_weight, filter_taps, filter_blocks, skip_gain):
    tokens, depth_here = activations.shape
    channels, out_tokens = filter_taps.shape
    tp_count, ctx_count = lax.axis_size("tp"), lax.axis_size("ctx")
    depth = 4
    width = channels // tp_count
    forward, inverse, twiddle = tables()

    def buffers(z_rows, z_lanes, x_rows, x_lanes):
        return [
            pltpu.VMEM((2, 2, z_rows, z_lanes), BF),
            pltpu.VMEM((2, 2, 2, z_rows, z_lanes), BF),
            pltpu.VMEM((2, z_rows, z_lanes), BF),
            pltpu.VMEM((4, 2, x_rows, x_lanes), BF),
            pltpu.VMEM((2, x_rows, x_lanes), BF),
            pltpu.VMEM((2, 2, x_rows, x_lanes), BF),
        ]

    tile = 2 * width
    n_tiles = 3 * channels // tile
    n_copies = (SETS + 1) * 28 + (1 + SETS) * (tp_count - 1) + (1 + 2 * SETS) * (ctx_count - 1)
    piece = width // SETS
    lanes = piece // ctx_count
    spec_rows = OUTER * lanes
    scratch = (
        [
            pltpu.VMEM((n_tiles, depth_here, tile), BF),
            pltpu.VMEM((tp_count, tokens, 2 * width), BF),
            pltpu.VMEM((tp_count, out_tokens, channels), BF),
        ]
        + buffers(ROWS_Z, piece, tokens - ROWS_Z, piece)
        + buffers(ROWS_Z, piece, tokens - ROWS_Z, piece)
        + buffers(out_tokens, LANES_Z // 2, out_tokens, (channels - LANES_Z) // 2)
        + [
            pltpu.VMEM((out_tokens, channels), BF),
            pltpu.VMEM((tokens, width), BF),
            pltpu.VMEM((SETS, piece, tokens), BF),
            pltpu.VMEM((ctx_count, SETS, lanes, tokens), BF),
            pltpu.VMEM((SETS, spec_rows, 2 * INNER), BF),
            pltpu.VMEM((SETS, spec_rows, 2 * INNER), F32),
            pltpu.VMEM((tokens, width), F32),
            pltpu.VMEM((SETS, piece, tokens), BF),
            pltpu.VMEM((SETS, ctx_count, lanes, tokens), BF),
            pltpu.VMEM((spec_rows, 2 * INNER), F32),
            pltpu.VMEM((SETS, ctx_count, lanes, tokens), BF),
            pltpu.VMEM((SETS, piece, tokens), BF),
            pltpu.VMEM((SETS, tokens, piece), BF),
            pltpu.VMEM((SETS, tp_count, out_tokens, piece), BF),
            pltpu.SemaphoreType.DMA((4 * n_tiles,)),
            pltpu.SemaphoreType.DMA((n_copies,)),
            pltpu.SemaphoreType.DMA((n_copies,)),
        ]
    )
    vmem = pl.BlockSpec(memory_space=pltpu.VMEM)
    out = pl.pallas_call(
        functools.partial(kernel, depth=depth, tp_count=tp_count, ctx_count=ctx_count),
        out_shape=jax.ShapeDtypeStruct((out_tokens, channels), BF),
        in_specs=[vmem, pl.BlockSpec(memory_space=pl.ANY)] + [vmem] * 6,
        out_specs=vmem,
        scratch_shapes=scratch,
        compiler_params=pltpu.CompilerParams(collective_id=0, has_side_effects=True, vmem_limit_bytes=60 * 2**20),
        name="hyena",
    )(
        activations,
        proj_weight,
        filter_taps.T,
        filter_blocks,
        skip_gain,
        jnp.asarray(forward),
        jnp.asarray(inverse),
        jnp.asarray(twiddle),
    )
    return out.T


def solution(mesh):
    placed = (P("ctx", "tp"), P("tp", None), P(None, ("ctx", "tp")), P(), P())
    return jax.shard_map(
        on_device, mesh=mesh, in_specs=placed, out_specs=P(None, ("ctx", "tp")), check_vma=False
    )
```

```python
import functools
import math

import jax
import jax.numpy as jnp
import ml_dtypes
import numpy as np
from jax import lax
from jax.experimental import pallas as pl
from jax.experimental.pallas import tpu as pltpu
from jax.sharding import PartitionSpec as P

BF = jnp.bfloat16
F32 = jnp.float32
OUTER = 32
INNER = 128
LENGTH = OUTER * INNER
SETS = 2
SHIFT = 0.25

ROWS_Z = 176
LANES_Z = 2816

SCHEDULE = (
    ("mm", 0, 2, 0), ("mm", 0, 2, 1), ("bar",), ("tap",), ("mm", 1, 2, 0), ("mm", 1, 2, 1), ("x1", 1, 2), ("z1", 0, 0),
    ("x1", 0, 2), ("mm", 0, 1, 0), ("mm", 0, 1, 1), ("z1", 1, 0), ("mm", 0, 3, 0), ("mm", 0, 3, 1), ("z1", 0, 1), ("mm", 1, 1, 0),
    ("mm", 1, 1, 1), ("x1", 0, 1), ("mm", 1, 3, 0), ("mm", 1, 3, 1), ("z2f", 0, 0, 1), ("x1", 1, 1), ("mm", 0, 0, 0),
    ("mm", 0, 0, 1), ("x1", 0, 3), ("drain", 5), ("pz1", 0, 0, 1), ("pz1", 0, 0, 0), ("mask",), ("z2f", 0, 0, 0), ("x1", 1, 3),
    ("mm", 1, 0, 0), ("mm", 1, 0, 1), ("tx1", 1, 2), ("z1", 1, 1), ("tx1", 0, 2), ("x2", 0), ("pz1", 1, 0, 1), ("drain", 16),
    ("zx", 0, 0), ("mq", 0), ("mq", 1), ("tx1", 0, 1), ("x2", 1), ("z2f", 0, 1, 1), ("mq", 2), ("mq", 3), ("z2f", 1, 0, 0),
    ("tx1", 0, 3), ("tx1", 1, 1), ("zx", 0, 1), ("x1", 1, 0), ("z2f", 1, 0, 1), ("pz1", 0, 1, 0), ("mq", 4), ("mq", 5),
    ("drain", 22), ("px2", 1, 0), ("mq", 6), ("mq", 7), ("px2", 0, 1), ("pz1", 0, 1, 1), ("pz1", 1, 0, 0), ("x3f", 0, 1),
    ("x3f", 0, 0), ("px2", 0, 0), ("tx1", 1, 3), ("z2f", 1, 1, 1), ("x1", 2, 2), ("z2f", 0, 1, 0), ("x1", 0, 0), ("filt",),
    ("x3f", 1, 1), ("px2", 1, 1), ("z2f", 1, 1, 0), ("pz1", 1, 1, 1), ("x3f", 1, 0), ("zx", 1, 1), ("drain", 41), ("zx", 1, 0),
    ("pz1", 1, 1, 0), ("x1", 2, 3), ("tx1", 2, 2), ("drain", 46), ("fin", 0), ("z1", 2, 0), ("z2f", 2, 0, 0), ("z1", 2, 1),
    ("gate", 0), ("x1", 2, 1), ("drain", 60), ("fin", 1), ("gate", 1), ("x2", 2), ("z2f", 2, 1, 0), ("pz1", 2, 0, 0),
    ("x1", 2, 0), ("pz1", 2, 0, 1), ("z2f", 2, 0, 1), ("drain", 64), ("conv", 0), ("tx1", 2, 3), ("pz1", 2, 1, 1), ("x3f", 2, 1),
    ("z2f", 2, 1, 1), ("tx1", 2, 1), ("drain", 70), ("conv", 1), ("zx", 2, 1), ("pz1", 2, 1, 0), ("drain", 74), ("home", 0),
    ("px2", 2, 0), ("zx", 2, 0), ("x3f", 2, 0), ("px2", 2, 1), ("drain", 82), ("home", 1), ("drain", 91), ("fin", 2), ("out",),
)


def flipped(index):
    return int(format(index, "05b")[::-1], 2)


def tables():
    at = np.arange(INNER)
    angle = 2.0 * math.pi * (at[:, None] * at[None, :] % INNER) / INNER
    cos, sin = np.cos(angle), np.sin(angle)
    forward = np.block([[cos, -sin], [sin, cos]])
    inverse = np.block([[cos, sin], [-sin, cos]])
    freqs = np.array([flipped(f) for f in range(OUTER)]) + SHIFT
    turn = 2.0 * math.pi * freqs[:, None] * at[None, :] / LENGTH

    def halves(matrix):
        high = matrix.astype(ml_dtypes.bfloat16)
        low = (matrix - high.astype(np.float64)).astype(ml_dtypes.bfloat16)
        return np.stack([high, low])

    twiddle = np.stack([np.cos(turn), np.sin(turn)]).astype(np.float32)
    return halves(forward), halves(inverse / LENGTH), twiddle


def times(pair, turn):
    re, im = pair
    turn = turn % 1.0
    if turn == 0.0:
        return pair
    if turn == 0.25:
        return (-im, re)
    if turn == 0.5:
        return (-re, -im)
    if turn == 0.75:
        return (im, -re)
    c, s = math.cos(2 * math.pi * turn), math.sin(2 * math.pi * turn)
    return (re * c - im * s, re * s + im * c)


def outer_forward(blocks):
    data = []
    for a, block in enumerate(blocks):
        angle = -2.0 * math.pi * a * SHIFT / OUTER
        data.append((block * math.cos(angle), block * math.sin(angle)) if a else (block, jnp.zeros_like(block)))
    half = OUTER // 2
    while half >= 1:
        for start in range(0, OUTER, 2 * half):
            for k in range(half):
                a, b = data[start + k], data[start + k + half]
                data[start + k] = (a[0] + b[0], a[1] + b[1])
                data[start + k + half] = times((a[0] - b[0], a[1] - b[1]), -k / (2 * half))
        half //= 2
    return data


def outer_inverse(data):
    data = list(data)
    half = 1
    while half < OUTER:
        for start in range(0, OUTER, 2 * half):
            for k in range(half):
                a, b = data[start + k], times(data[start + k + half], k / (2 * half))
                data[start + k] = (a[0] + b[0], a[1] + b[1])
                data[start + k + half] = (a[0] - b[0], a[1] - b[1])
        half *= 2
    out = []
    for a, (re, im) in enumerate(data):
        angle = 2.0 * math.pi * a * SHIFT / OUTER
        out.append(re * math.cos(angle) - im * math.sin(angle))
    return out


class Spread:
    def __init__(self, place, links, part, bufs):
        self.place, self.links, self.part = place, links, part
        self.z1, self.z2, self.zx, self.x1, self.x2, self.x3 = bufs
        self.pending = {}

    def cell(self, own, step, piece, half):
        return self.part(self.place.owner(own, step), piece, half)

    def send(self, key, src, dst, to):
        self.pending[key] = self.links.send(src, dst, to)

    def start_z1(self, own):
        for way in (0, 1):
            self.send(("z1", own, way), self.cell(own, 2, 0, way), self.z1.at[way, own], self.place.zway[way])

    def start_x1(self, step):
        for half in (0, 1):
            self.send(("x1", step, half), self.cell(0, step, 1, half), self.x1.at[step, half], self.place.far)

    def start_z2_free(self, own, way):
        step = (1, 3)[way]
        self.send(("z2", own, way, 1 - way), self.cell(own, step, 0, 1 - way), self.z2.at[way, own, 1 - way], self.place.zway[way])

    def pass_z1(self, own, way):
        self.pending[("z1", own, way)].wait_recv()
        cell = self.cell(own, (1, 3)[way], 0, way)
        cell[...] = (cell[...].astype(F32) + self.z1[way, own].astype(F32)).astype(BF)
        self.send(("z2", own, way, way), cell, self.z2.at[way, own, way], self.place.zway[way])

    def take_x1(self, step):
        for half in (0, 1):
            self.pending[("x1", step, half)].wait_recv()
            cell = self.cell(1, step, 1, half)
            cell[...] = (cell[...].astype(F32) + self.x1[step, half].astype(F32)).astype(BF)

    def start_x2(self):
        for way in (0, 1):
            self.send(("x2", way), self.cell(1, 2, 1, way), self.x2.at[way], self.place.zway[way])

    def start_x3_free(self, way):
        self.send(("x3", way, 1 - way), self.cell(1, (1, 3)[way], 1, 1 - way), self.x3.at[way, 1 - way], self.place.zway[way])

    def pass_x2(self, way):
        self.pending[("x2", way)].wait_recv()
        cell = self.cell(1, (1, 3)[way], 1, way)
        cell[...] = (cell[...].astype(F32) + self.x2[way].astype(F32)).astype(BF)
        self.send(("x3", way, way), cell, self.x3.at[way, way], self.place.zway[way])

    def start_zx(self, half):
        for way in (0, 1):
            self.pending[("z2", 0, way, half)].wait_recv()
        cell = self.cell(0, 0, 0, half)
        total = cell[...].astype(F32) + self.z2[0, 0, half].astype(F32) + self.z2[1, 0, half].astype(F32)
        cell[...] = total.astype(BF)
        self.send(("zx", half), cell, self.zx.at[half], self.place.far)

    def finish(self):
        for half in (0, 1):
            self.pending[("x1", 0, half)].wait_recv()
            for way in (0, 1):
                self.pending[("z2", 1, way, half)].wait_recv()
                self.pending[("x3", way, half)].wait_recv()
            self.pending[("zx", half)].wait_recv()

    def total(self, piece, half):
        mine = self.cell(1, 0, piece, half)[...].astype(F32)
        if piece == 0:
            terms = (self.z2[0, 1, half], self.z2[1, 1, half], self.zx[half])
        else:
            terms = (self.x1[0, half], self.x3[0, half], self.x3[1, half])
        for term in terms:
            mine = mine + term.astype(F32)
        return mine


class Place:
    def __init__(self, depth, tp_count, ctx_count):
        self.ctx, self.tp = lax.axis_index("ctx"), lax.axis_index("tp")
        self.depth, self.tp_count, self.ctx_count = depth, tp_count, ctx_count
        self.x_half, self.z = self.tp // depth, self.tp % depth
        self.zway = tuple((self.ctx, self.x_half * depth + (self.z + step) % depth) for step in (1, depth - 1))
        self.far = (self.ctx, (self.tp + depth) % tp_count)

    def owner(self, own, step):
        half = self.x_half if own else 1 - self.x_half
        return half * self.depth + (self.z + step) % self.depth


class Links:
    def __init__(self, send_sems, recv_sems):
        self.send_sems, self.recv_sems = send_sems, recv_sems
        self.used = 0
        self.drained = 0
        self.started = []

    def make(self, src, dst, to, at):
        return pltpu.make_async_remote_copy(
            src_ref=src,
            dst_ref=dst,
            send_sem=self.send_sems.at[at],
            recv_sem=self.recv_sems.at[at],
            device_id=to,
            device_id_type=pl.DeviceIdType.MESH,
        )

    def send(self, src, dst, to):
        copy = self.make(src, dst, to, self.used)
        self.used += 1
        copy.start()
        self.started.append(copy)
        return copy

    def drain(self, count):
        for at in range(self.drained, count):
            self.started[at].wait_send()
        self.drained = max(self.drained, count)


class Swap:
    def __init__(self, links, count, me, device, src, dst):
        self.links, self.count, self.me, self.device, self.src, self.dst = links, count, me, device, src, dst
        self.base = links.used
        links.used += count - 1

    def copy(self, away):
        peer = (self.me + away) % self.count
        return self.links.make(self.src(peer), self.dst(self.me), self.device(peer), self.base + away - 1)

    def each(self, act):
        lax.fori_loop(1, self.count, lambda away, carry: (act(self.copy(away)), carry)[1], 0)

    def start(self):
        self.each(lambda copy: copy.start())
        self.links.started.append(self)

    def wait_recv(self):
        self.each(lambda copy: copy.wait_recv())

    def wait_send(self):
        self.each(lambda copy: copy.wait_send())


def transposed(source, target, rows, lanes):
    for r in range(0, rows, 128):
        for c in range(0, lanes, 128):
            tile = source[pl.ds(r, 128), pl.ds(c, 128)].astype(F32)
            target[pl.ds(c, 128), pl.ds(r, 128)] = tile.T.astype(target.dtype)


def spectrum(source, staged, twiddle):
    ctx_count, lanes, span = source.shape
    blocks = []
    for i in range(ctx_count):
        for u in range(span // INNER):
            blocks.append(source[i, :, pl.ds(u * INNER, INNER)].astype(F32))
    for f, (re, im) in enumerate(outer_forward(blocks)):
        c, s = twiddle[0, pl.ds(f, 1), :], twiddle[1, pl.ds(f, 1), :]
        staged[pl.ds(f * lanes, lanes), pl.ds(0, INNER)] = (re * c + im * s).astype(BF)
        staged[pl.ds(f * lanes, lanes), pl.ds(INNER, INNER)] = (im * c - re * s).astype(BF)


def both(data, matrix):
    return jnp.dot(data, matrix[0], preferred_element_type=F32) + jnp.dot(data, matrix[1], preferred_element_type=F32)


def kernel(
    act_hbm, weight, taps_hbm, blocks_hbm, gains_hbm, forward_hbm, inverse_hbm, twiddle_hbm,
    out,
    act, taps, blocks, gains, forward, inverse, twiddle,
    wbuf, kv, qs,
    a_z1, a_z2, a_zx, a_x1, a_x2, a_x3,
    b_z1, b_z2, b_zx, b_x1, b_x2, b_x3,
    q_z1, q_z2, q_zx, q_x1, q_x2, q_x3,
    taps_out, taps_in, taps_t, filt_in, staged, filt_spec,
    gated, gated_t, gated_in, mixed, conv_out, conv_in, conv_home, conv_final,
    w_sems, in_sems, send_sems, recv_sems,
    *, depth, tp_count, ctx_count,
):
    place = Place(depth, tp_count, ctx_count)
    me, tp = place.ctx, place.tp
    tokens, width = gated.shape
    out_tokens = tokens // tp_count
    channels = tp_count * width
    tile = wbuf.shape[2]
    piece = width // SETS
    lanes = piece // ctx_count

    order = [step[1:] for step in SCHEDULE if step[0] == "mm"]
    tiles = []
    for own, step, c in order:
        base = place.owner(own, step) * width + c * piece
        tiles.append([(which * channels + base, piece) for which in (1, 2)])
    for t in range(channels // tile):
        tiles.append([(t * tile, tile)])

    def fetch(t, act_on):
        at = 0
        for k, (column, size) in enumerate(tiles[t]):
            src = weight.at[:, pl.ds(pl.multiple_of(column, size), size)]
            act_on(pltpu.make_async_copy(src, wbuf.at[t, :, pl.ds(at, size)], w_sems.at[2 * t + k]))
            at += size

    barrier = pltpu.get_barrier_semaphore()

    def greet(device):
        pl.semaphore_signal(barrier, inc=1, device_id=device, device_id_type=pl.DeviceIdType.MESH)

    greet(place.far)
    for step in range(1, depth):
        greet((me, place.owner(1, step)))
    for step in range(1, depth):
        greet((me, place.owner(0, step)))
    for away in range(1, ctx_count):
        greet(((me + away) % ctx_count, tp))

    pairs = ((act_hbm, act), (taps_hbm, taps), (blocks_hbm, blocks), (gains_hbm, gains),
             (forward_hbm, forward), (inverse_hbm, inverse), (twiddle_hbm, twiddle))
    inputs = [pltpu.make_async_copy(source, target, in_sems.at[k]) for k, (source, target) in enumerate(pairs)]
    inputs[0].start()
    fetch(0, lambda copy: copy.start())
    inputs[1].start()

    ahead = 6
    for t in range(1, ahead):
        fetch(t, lambda copy: copy.start())
    for copy in inputs[2:]:
        copy.start()

    def next_tile(t):
        fetch(t, lambda copy: copy.wait())
        if t + ahead < len(tiles):
            fetch(t + ahead, lambda copy: copy.start())

    inputs[1].wait()
    taps_out[...] = taps[...].astype(BF)
    inputs[0].wait()

    links = Links(send_sems, recv_sems)

    def over_tp(src, dst):
        return Swap(links, tp_count, tp, lambda peer: (me, peer), src, dst)

    def over_ctx(src, dst):
        return Swap(links, ctx_count, me, lambda peer: (peer, tp), src, dst)

    def span(index, size):
        return pl.ds(pl.multiple_of(index * size, size), size)

    tap_swap = over_tp(lambda peer: taps_out.at[:, span(peer, width)], lambda mine: taps_in.at[span(mine, out_tokens)])
    filt_swap = over_ctx(lambda peer: taps_t.at[:, span(peer, lanes)], lambda mine: filt_in.at[mine])
    gated_swap = [over_ctx(lambda peer, c=c: gated_t.at[c, span(peer, lanes)], lambda mine, c=c: gated_in.at[c, mine]) for c in range(SETS)]
    conv_swap = [over_ctx(lambda peer, c=c: conv_out.at[c, peer], lambda mine, c=c: conv_in.at[c, span(mine, lanes)]) for c in range(SETS)]
    home_swap = [over_tp(lambda peer, c=c: conv_home.at[c, span(peer, out_tokens)], lambda mine, c=c: conv_final.at[c, mine]) for c in range(SETS)]

    def kv_part(c):
        def part(owner, which, half):
            rows = pl.ds(0, ROWS_Z) if which == 0 else pl.ds(ROWS_Z, tokens - ROWS_Z)
            return kv.at[owner, rows, pl.ds((2 * c + half) * piece, piece)]
        return part

    z_half, x_half = LANES_Z // 2, (channels - LANES_Z) // 2

    def q_part(owner, which, half):
        return qs.at[owner, :, pl.ds(half * z_half, z_half) if which == 0 else pl.ds(LANES_Z + half * x_half, x_half)]

    spreads = (
        Spread(place, links, kv_part(0), (a_z1, a_z2, a_zx, a_x1, a_x2, a_x3)),
        Spread(place, links, kv_part(1), (b_z1, b_z2, b_zx, b_x1, b_x2, b_x3)),
        Spread(place, links, q_part, (q_z1, q_z2, q_zx, q_x1, q_x2, q_x3)),
    )

    def multiply_kv(own, step, c):
        t = order.index((own, step, c))
        next_tile(t)
        block = jnp.dot(act[...], wbuf[t], preferred_element_type=F32)
        kv[place.owner(own, step), :, pl.ds(c * tile, tile)] = block.astype(BF)

    def multiply_q(t):
        next_tile(len(order) + t)
        block = jnp.dot(act[...], wbuf[len(order) + t], preferred_element_type=F32).astype(BF)
        qs[:, :, pl.ds(t * tile, tile)] = block.reshape(tp_count, out_tokens, tile)

    def mask():
        tap_swap.wait_recv()
        taps_in[span(tp, out_tokens), :] = taps_out[:, span(tp, width)]
        for copy in inputs[2:]:
            copy.wait()
        live = me < blocks[span(tp, width)].reshape(1, width)
        for c in range(SETS):
            for r in range(0, tokens, 128):
                for k in range(0, piece, 128):
                    at = c * piece + k
                    block = taps_in[pl.ds(r, 128), pl.ds(at, 128)].astype(F32)
                    block = jnp.where(live[:, at:at + 128], block, 0.0)
                    taps_t[c, pl.ds(k, 128), pl.ds(r, 128)] = block.T.astype(BF)
        filt_swap.start()

    rows = staged.shape[1] // 2

    def filter_spectrum():
        filt_swap.wait_recv()
        filt_in[me] = taps_t[:, span(me, lanes), :]
        for c in range(SETS):
            spectrum(filt_in.at[:, c], staged.at[c], twiddle)
            for n in range(2):
                at = pl.ds(n * rows, rows)
                filt_spec[c, at, :] = both(staged[c, at, :], forward)

    def finish(c):
        spreads[c].finish()
        if c < SETS:
            for which, at in ((0, pl.ds(0, ROWS_Z)), (1, pl.ds(ROWS_Z, tokens - ROWS_Z))):
                gated[at, pl.ds(c * piece, piece)] = spreads[c].total(which, 0) * spreads[c].total(which, 1)

    def gate(c):
        transposed(gated.at[:, pl.ds(c * piece, piece)], gated_t.at[c], tokens, piece)
        gated_swap[c].start()

    def convolve(c):
        gated_swap[c].wait_recv()
        gated_in[c, me] = gated_t[c, span(me, lanes), :]
        spectrum(gated_in.at[c], staged.at[c], twiddle)
        for n in range(2):
            at = pl.ds(n * rows, rows)
            a, b = both(staged[c, at, :], forward), filt_spec[c, at, :]
            a_re, a_im, b_re, b_im = a[:, :INNER], a[:, INNER:], b[:, :INNER], b[:, INNER:]
            prod = jnp.concatenate([a_re * b_re - a_im * b_im, a_re * b_im + a_im * b_re], axis=1)
            mixed[at, :] = both(prod.astype(BF), inverse)
        data = []
        for f in range(OUTER):
            cos, sin = twiddle[0, pl.ds(f, 1), :], twiddle[1, pl.ds(f, 1), :]
            row = pl.ds(f * lanes, lanes)
            re, im = mixed[row, pl.ds(0, INNER)], mixed[row, pl.ds(INNER, INNER)]
            data.append((re * cos - im * sin, re * sin + im * cos))
        fold = tokens // INNER
        for a, block in enumerate(outer_inverse(data)):
            conv_out[c, a // fold, :, pl.ds(a % fold * INNER, INNER)] = block.astype(BF)
        conv_swap[c].start()

    def home(c):
        conv_swap[c].wait_recv()
        conv_in[c, span(me, lanes), :] = conv_out[c, me]
        gain = gains[span(tp, width)].reshape(1, width)
        for r in range(0, tokens, 128):
            for k in range(0, piece, 128):
                at = c * piece + k
                conv = conv_in[c, pl.ds(k, 128), pl.ds(r, 128)].astype(F32).T
                total = conv + gain[:, at:at + 128] * gated[pl.ds(r, 128), pl.ds(at, 128)]
                conv_home[c, pl.ds(r, 128), pl.ds(k, 128)] = total.astype(BF)
        home_swap[c].start()

    def finale():
        for c in range(SETS):
            home_swap[c].wait_recv()
            conv_final[c, tp] = conv_home[c, span(tp, out_tokens), :]
        query = jnp.concatenate([spreads[SETS].total(which, half) for which in (0, 1) for half in (0, 1)], axis=1)
        for j in range(tp_count):
            for c in range(SETS):
                at = slice(j * width + c * piece, j * width + (c + 1) * piece)
                out[:, at] = (query[:, at] * conv_final[c, j].astype(F32)).astype(BF)

    steps = {
        "bar": lambda: pl.semaphore_wait(barrier, tp_count + ctx_count - 2),
        "mm": multiply_kv,
        "mq": multiply_q,
        "tap": tap_swap.start,
        "mask": mask,
        "filt": filter_spectrum,
        "z1": lambda c, own: spreads[c].start_z1(own),
        "x1": lambda c, step: spreads[c].start_x1(step),
        "z2f": lambda c, own, way: spreads[c].start_z2_free(own, way),
        "pz1": lambda c, own, way: spreads[c].pass_z1(own, way),
        "tx1": lambda c, step: spreads[c].take_x1(step),
        "x2": lambda c: spreads[c].start_x2(),
        "x3f": lambda c, way: spreads[c].start_x3_free(way),
        "px2": lambda c, way: spreads[c].pass_x2(way),
        "zx": lambda c, half: spreads[c].start_zx(half),
        "fin": finish,
        "gate": gate,
        "conv": convolve,
        "home": home,
        "out": finale,
        "drain": links.drain,
    }
    for step in SCHEDULE:
        steps[step[0]](*step[1:])

    links.drain(len(links.started))


def on_device(activations, proj_weight, filter_taps, filter_blocks, skip_gain):
    tokens, depth_here = activations.shape
    channels, out_tokens = filter_taps.shape
    tp_count, ctx_count = lax.axis_size("tp"), lax.axis_size("ctx")
    depth = 4
    width = channels // tp_count
    forward, inverse, twiddle = tables()

    def buffers(z_rows, z_lanes, x_rows, x_lanes):
        return [
            pltpu.VMEM((2, 2, z_rows, z_lanes), BF),
            pltpu.VMEM((2, 2, 2, z_rows, z_lanes), BF),
            pltpu.VMEM((2, z_rows, z_lanes), BF),
            pltpu.VMEM((4, 2, x_rows, x_lanes), BF),
            pltpu.VMEM((2, x_rows, x_lanes), BF),
            pltpu.VMEM((2, 2, x_rows, x_lanes), BF),
        ]

    tile = width
    n_tiles = 3 * channels // tile
    n_copies = (SETS + 1) * 28 + (1 + SETS) * (tp_count - 1) + (1 + 2 * SETS) * (ctx_count - 1)
    piece = width // SETS
    lanes = piece // ctx_count
    spec_rows = OUTER * lanes
    scratch = (
        [
            pltpu.VMEM((tokens, depth_here), BF),
            pltpu.VMEM((out_tokens, channels), F32),
            pltpu.VMEM((channels,), jnp.int32),
            pltpu.VMEM((channels,), F32),
            pltpu.VMEM(forward.shape, BF),
            pltpu.VMEM(inverse.shape, BF),
            pltpu.VMEM(twiddle.shape, F32),
            pltpu.VMEM((n_tiles, depth_here, tile), BF),
            pltpu.VMEM((tp_count, tokens, 2 * width), BF),
            pltpu.VMEM((tp_count, out_tokens, channels), BF),
        ]
        + buffers(ROWS_Z, piece, tokens - ROWS_Z, piece)
        + buffers(ROWS_Z, piece, tokens - ROWS_Z, piece)
        + buffers(out_tokens, LANES_Z // 2, out_tokens, (channels - LANES_Z) // 2)
        + [
            pltpu.VMEM((out_tokens, channels), BF),
            pltpu.VMEM((tokens, width), BF),
            pltpu.VMEM((SETS, piece, tokens), BF),
            pltpu.VMEM((ctx_count, SETS, lanes, tokens), BF),
            pltpu.VMEM((SETS, spec_rows, 2 * INNER), BF),
            pltpu.VMEM((SETS, spec_rows, 2 * INNER), F32),
            pltpu.VMEM((tokens, width), F32),
            pltpu.VMEM((SETS, piece, tokens), BF),
            pltpu.VMEM((SETS, ctx_count, lanes, tokens), BF),
            pltpu.VMEM((spec_rows, 2 * INNER), F32),
            pltpu.VMEM((SETS, ctx_count, lanes, tokens), BF),
            pltpu.VMEM((SETS, piece, tokens), BF),
            pltpu.VMEM((SETS, tokens, piece), BF),
            pltpu.VMEM((SETS, tp_count, out_tokens, piece), BF),
            pltpu.SemaphoreType.DMA((2 * n_tiles,)),
            pltpu.SemaphoreType.DMA((7,)),
            pltpu.SemaphoreType.DMA((n_copies,)),
            pltpu.SemaphoreType.DMA((n_copies,)),
        ]
    )
    vmem = pl.BlockSpec(memory_space=pltpu.VMEM)
    out = pl.pallas_call(
        functools.partial(kernel, depth=depth, tp_count=tp_count, ctx_count=ctx_count),
        out_shape=jax.ShapeDtypeStruct((out_tokens, channels), BF),
        in_specs=[pl.BlockSpec(memory_space=pl.ANY)] * 8,
        out_specs=vmem,
        scratch_shapes=scratch,
        compiler_params=pltpu.CompilerParams(collective_id=0, has_side_effects=True, vmem_limit_bytes=60 * 2**20),
        name="hyena",
    )(
        activations,
        proj_weight,
        filter_taps.T,
        filter_blocks,
        skip_gain,
        jnp.asarray(forward),
        jnp.asarray(inverse),
        jnp.asarray(twiddle),
    )
    return out.T


def solution(mesh):
    placed = (P("ctx", "tp"), P("tp", None), P(None, ("ctx", "tp")), P(), P())
    return jax.shard_map(
        on_device, mesh=mesh, in_specs=placed, out_specs=P(None, ("ctx", "tp")), check_vma=False
    )
```

```python
import functools
import math

import jax
import jax.numpy as jnp
import ml_dtypes
import numpy as np
from jax import lax
from jax.experimental import pallas as pl
from jax.experimental.pallas import tpu as pltpu
from jax.sharding import PartitionSpec as P

BF = jnp.bfloat16
F32 = jnp.float32
OUTER = 32
INNER = 128
LENGTH = OUTER * INNER
SIDES = 2
SETS = 2
SHIFT = 0.25

ROWS_Z = 160
LANES_Z = 2560

SCHEDULE = (
    ("mm", 0, 3, 0), ("mm", 1, 2, 1), ("mm", 0, 2, 0), ("bar",), ("tap",), ("mm", 0, 3, 1), ("mm", 0, 2, 1), ("z1", 1, 1),
    ("mm", 0, 0, 1), ("x1", 0, 3), ("mm", 1, 2, 0), ("z1", 0, 0), ("x1", 1, 0), ("z2f", 0, 0, 1), ("mm", 0, 1, 0), ("z1", 1, 0),
    ("mm", 0, 0, 0), ("mm", 0, 1, 1), ("x1", 0, 2), ("mm", 1, 3, 0), ("z2f", 1, 0, 0), ("z2f", 1, 0, 1), ("x1", 1, 2),
    ("mm", 1, 0, 0), ("z1", 0, 1), ("mm", 1, 1, 0), ("mask",), ("x1", 0, 1), ("z2f", 0, 0, 0), ("mm", 1, 0, 1), ("x1", 1, 3),
    ("mm", 1, 3, 1), ("drain", 7), ("pz1", 0, 0, 1), ("pz1", 1, 0, 0), ("tx1", 0, 3), ("x3f", 0, 1), ("x1", 1, 1),
    ("mm", 1, 1, 1), ("x1", 0, 0), ("pz1", 1, 1, 1), ("pz1", 0, 0, 0), ("mq", 0), ("tx1", 0, 2), ("x2", 0), ("mq", 1),
    ("drain", 18), ("tx1", 1, 2), ("x2", 1), ("pz1", 1, 1, 0), ("drain", 24), ("tx1", 0, 1), ("pz1", 1, 0, 1), ("mq", 2),
    ("pz1", 0, 1, 0), ("z2f", 0, 1, 0), ("mq", 3), ("mq", 4), ("zx", 1, 0), ("mq", 5), ("drain", 29), ("zx", 0, 0),
    ("pz1", 0, 1, 1), ("zx", 0, 1), ("tx1", 1, 3), ("z2f", 0, 1, 1), ("filt",), ("z2f", 1, 1, 0), ("mq", 6), ("tx1", 1, 1),
    ("x3f", 0, 0), ("px2", 0, 0), ("px2", 0, 1), ("px2", 1, 1), ("drain", 42), ("zx", 1, 1), ("mq", 7), ("px2", 1, 0),
    ("x1", 2, 3), ("x3f", 1, 1), ("z2f", 1, 1, 1), ("x1", 2, 2), ("x3f", 1, 0), ("z1", 2, 0), ("z1", 2, 1), ("z2f", 2, 0, 0),
    ("z2f", 2, 0, 1), ("drain", 54), ("fin", 0), ("gate", 0), ("drain", 62), ("fin", 1), ("gate", 1), ("x1", 2, 1),
    ("pz1", 2, 0, 1), ("x1", 2, 0), ("tx1", 2, 2), ("pz1", 2, 0, 0), ("x2", 2), ("tx1", 2, 3), ("z2f", 2, 1, 1), ("drain", 66),
    ("pz1", 2, 1, 0), ("z2f", 2, 1, 0), ("conv", 0), ("drain", 70), ("conv", 1), ("zx", 2, 1), ("x3f", 2, 1), ("tx1", 2, 1),
    ("x3f", 2, 0), ("zx", 2, 0), ("pz1", 2, 1, 1), ("drain", 80), ("home", 0), ("px2", 2, 0), ("px2", 2, 1), ("drain", 86),
    ("home", 1), ("drain", 91), ("fin", 2), ("out",),
)


def flipped(index):
    return int(format(index, "05b")[::-1], 2)


def tables():
    at = np.arange(INNER)
    angle = 2.0 * math.pi * (at[:, None] * at[None, :] % INNER) / INNER
    cos, sin = np.cos(angle), np.sin(angle)
    forward = np.block([[cos, -sin], [sin, cos]])
    inverse = np.block([[cos, sin], [-sin, cos]])
    freqs = np.array([flipped(f) for f in range(OUTER)]) + SHIFT
    turn = 2.0 * math.pi * freqs[:, None] * at[None, :] / LENGTH

    def halves(matrix):
        high = matrix.astype(ml_dtypes.bfloat16)
        low = (matrix - high.astype(np.float64)).astype(ml_dtypes.bfloat16)
        return np.stack([high, low])

    twiddle = np.stack([np.cos(turn), np.sin(turn)]).astype(np.float32)
    return halves(forward), halves(inverse / LENGTH), twiddle


def times(pair, turn):
    re, im = pair
    turn = turn % 1.0
    if turn == 0.0:
        return pair
    if turn == 0.25:
        return (-im, re)
    if turn == 0.5:
        return (-re, -im)
    if turn == 0.75:
        return (im, -re)
    c, s = math.cos(2 * math.pi * turn), math.sin(2 * math.pi * turn)
    return (re * c - im * s, re * s + im * c)


def outer_forward(blocks):
    data = []
    for a, block in enumerate(blocks):
        angle = -2.0 * math.pi * a * SHIFT / OUTER
        data.append((block * math.cos(angle), block * math.sin(angle)) if a else (block, jnp.zeros_like(block)))
    half = OUTER // 2
    while half >= 1:
        for start in range(0, OUTER, 2 * half):
            for k in range(half):
                a, b = data[start + k], data[start + k + half]
                data[start + k] = (a[0] + b[0], a[1] + b[1])
                data[start + k + half] = times((a[0] - b[0], a[1] - b[1]), -k / (2 * half))
        half //= 2
    return data


def outer_inverse(data):
    data = list(data)
    half = 1
    while half < OUTER:
        for start in range(0, OUTER, 2 * half):
            for k in range(half):
                a, b = data[start + k], times(data[start + k + half], k / (2 * half))
                data[start + k] = (a[0] + b[0], a[1] + b[1])
                data[start + k + half] = (a[0] - b[0], a[1] - b[1])
        half *= 2
    out = []
    for a, (re, im) in enumerate(data):
        angle = 2.0 * math.pi * a * SHIFT / OUTER
        out.append(re * math.cos(angle) - im * math.sin(angle))
    return out


class Spread:
    def __init__(self, place, links, part, bufs):
        self.place, self.links, self.part = place, links, part
        self.z1, self.z2, self.zx, self.x1, self.x2, self.x3 = bufs
        self.pending = {}

    def cell(self, own, step, piece, half):
        return self.part(self.place.owner(own, step), piece, half)

    def send(self, key, src, dst, to):
        self.pending[key] = self.links.send(src, dst, to)

    def start_z1(self, own):
        for way in (0, 1):
            self.send(("z1", own, way), self.cell(own, 2, 0, way), self.z1.at[way, own], self.place.zway[way])

    def start_x1(self, step):
        for half in (0, 1):
            self.send(("x1", step, half), self.cell(0, step, 1, half), self.x1.at[step, half], self.place.far)

    def start_z2_free(self, own, way):
        step = (1, 3)[way]
        self.send(("z2", own, way, 1 - way), self.cell(own, step, 0, 1 - way), self.z2.at[way, own, 1 - way], self.place.zway[way])

    def pass_z1(self, own, way):
        self.pending[("z1", own, way)].wait_recv()
        cell = self.cell(own, (1, 3)[way], 0, way)
        cell[...] = (cell[...].astype(F32) + self.z1[way, own].astype(F32)).astype(BF)
        self.send(("z2", own, way, way), cell, self.z2.at[way, own, way], self.place.zway[way])

    def take_x1(self, step):
        for half in (0, 1):
            self.pending[("x1", step, half)].wait_recv()
            cell = self.cell(1, step, 1, half)
            cell[...] = (cell[...].astype(F32) + self.x1[step, half].astype(F32)).astype(BF)

    def start_x2(self):
        for way in (0, 1):
            self.send(("x2", way), self.cell(1, 2, 1, way), self.x2.at[way], self.place.zway[way])

    def start_x3_free(self, way):
        self.send(("x3", way, 1 - way), self.cell(1, (1, 3)[way], 1, 1 - way), self.x3.at[way, 1 - way], self.place.zway[way])

    def pass_x2(self, way):
        self.pending[("x2", way)].wait_recv()
        cell = self.cell(1, (1, 3)[way], 1, way)
        cell[...] = (cell[...].astype(F32) + self.x2[way].astype(F32)).astype(BF)
        self.send(("x3", way, way), cell, self.x3.at[way, way], self.place.zway[way])

    def start_zx(self, half):
        for way in (0, 1):
            self.pending[("z2", 0, way, half)].wait_recv()
        cell = self.cell(0, 0, 0, half)
        total = cell[...].astype(F32) + self.z2[0, 0, half].astype(F32) + self.z2[1, 0, half].astype(F32)
        cell[...] = total.astype(BF)
        self.send(("zx", half), cell, self.zx.at[half], self.place.far)

    def finish(self):
        for half in (0, 1):
            self.pending[("x1", 0, half)].wait_recv()
            for way in (0, 1):
                self.pending[("z2", 1, way, half)].wait_recv()
                self.pending[("x3", way, half)].wait_recv()
            self.pending[("zx", half)].wait_recv()

    def total(self, piece, half):
        mine = self.cell(1, 0, piece, half)[...].astype(F32)
        if piece == 0:
            terms = (self.z2[0, 1, half], self.z2[1, 1, half], self.zx[half])
        else:
            terms = (self.x1[0, half], self.x3[0, half], self.x3[1, half])
        for term in terms:
            mine = mine + term.astype(F32)
        return mine


class Place:
    def __init__(self, depth, tp_count, ctx_count):
        self.ctx, self.tp = lax.axis_index("ctx"), lax.axis_index("tp")
        self.depth, self.tp_count, self.ctx_count = depth, tp_count, ctx_count
        self.x_half, self.z = self.tp // depth, self.tp % depth
        self.zway = tuple((self.ctx, self.x_half * depth + (self.z + step) % depth) for step in (1, depth - 1))
        self.far = (self.ctx, (self.tp + depth) % tp_count)

    def owner(self, own, step):
        half = self.x_half if own else 1 - self.x_half
        return half * self.depth + (self.z + step) % self.depth


class Links:
    def __init__(self, send_sems, recv_sems):
        self.send_sems, self.recv_sems = send_sems, recv_sems
        self.used = 0
        self.drained = 0
        self.started = []

    def make(self, src, dst, to, at):
        return pltpu.make_async_remote_copy(
            src_ref=src,
            dst_ref=dst,
            send_sem=self.send_sems.at[at],
            recv_sem=self.recv_sems.at[at],
            device_id=to,
            device_id_type=pl.DeviceIdType.MESH,
        )

    def send(self, src, dst, to):
        copy = self.make(src, dst, to, self.used)
        self.used += 1
        copy.start()
        self.started.append(copy)
        return copy

    def drain(self, count):
        for at in range(self.drained, count):
            self.started[at].wait_send()
        self.drained = max(self.drained, count)


class Swap:
    def __init__(self, links, count, me, device, src, dst):
        self.links, self.count, self.me, self.device, self.src, self.dst = links, count, me, device, src, dst
        self.base = links.used
        links.used += count - 1

    def copy(self, away):
        peer = (self.me + away) % self.count
        return self.links.make(self.src(peer), self.dst(self.me), self.device(peer), self.base + away - 1)

    def each(self, act):
        lax.fori_loop(1, self.count, lambda away, carry: (act(self.copy(away)), carry)[1], 0)

    def start(self):
        self.each(lambda copy: copy.start())
        self.links.started.append(self)

    def wait_recv(self):
        self.each(lambda copy: copy.wait_recv())

    def wait_send(self):
        self.each(lambda copy: copy.wait_send())


def transposed(source, target, rows, lanes):
    for r in range(0, rows, 128):
        for c in range(0, lanes, 128):
            tile = source[pl.ds(r, 128), pl.ds(c, 128)].astype(F32)
            target[pl.ds(c, 128), pl.ds(r, 128)] = tile.T.astype(target.dtype)


def spectrum(blocks, staged, twiddle):
    lanes = blocks[0].shape[0]
    for f, (re, im) in enumerate(outer_forward([block.astype(F32) for block in blocks])):
        c, s = twiddle[0, pl.ds(f, 1), :], twiddle[1, pl.ds(f, 1), :]
        staged[pl.ds(f * lanes, lanes), pl.ds(0, INNER)] = (re * c + im * s).astype(BF)
        staged[pl.ds(f * lanes, lanes), pl.ds(INNER, INNER)] = (im * c - re * s).astype(BF)


def both(data, matrix):
    return jnp.dot(data, matrix[0], preferred_element_type=F32) + jnp.dot(data, matrix[1], preferred_element_type=F32)


def kernel(
    act_hbm, weight, taps_hbm, blocks_hbm, gains_hbm, forward_hbm, inverse_hbm, twiddle_hbm,
    out,
    act, taps, blocks, gains, forward, inverse, twiddle,
    wbuf, kv, qs,
    a_z1, a_z2, a_zx, a_x1, a_x2, a_x3,
    b_z1, b_z2, b_zx, b_x1, b_x2, b_x3,
    q_z1, q_z2, q_zx, q_x1, q_x2, q_x3,
    taps_out, taps_in, taps_t, filt_in, staged, filt_spec, gain_t,
    gated, gated_t, gated_in, mixed, conv_out, conv_in, conv_home, conv_final,
    w_sems, in_sems, send_sems, recv_sems,
    *, depth, tp_count, ctx_count,
):
    place = Place(depth, tp_count, ctx_count)
    me, tp = place.ctx, place.tp
    tokens, width = gated.shape
    out_tokens = tokens // tp_count
    channels = tp_count * width
    tile = wbuf.shape[2]
    piece = width // SETS
    lanes = piece // ctx_count
    spots = ctx_count // SIDES
    part = lanes * spots
    side, spot = me // spots, me % spots
    crowd = SIDES * tp_count

    order = [step[1:] for step in SCHEDULE if step[0] == "mm"]
    tiles = []
    for own, step, c in order:
        base = place.owner(own, step) * width + c * part
        tiles.append([(which * channels + base + side * piece, part) for which in (1, 2) for side in range(SIDES)])
    for t in range(channels // tile):
        tiles.append([(t * tile, tile)])

    def fetch(t, act_on):
        at = 0
        for k, (column, size) in enumerate(tiles[t]):
            src = weight.at[:, pl.ds(pl.multiple_of(column, size), size)]
            act_on(pltpu.make_async_copy(src, wbuf.at[t, :, pl.ds(at, size)], w_sems.at[4 * t + k]))
            at += size

    barrier = pltpu.get_barrier_semaphore()

    def greet(device):
        pl.semaphore_signal(barrier, inc=1, device_id=device, device_id_type=pl.DeviceIdType.MESH)

    def across(away):
        return (me + away) % ctx_count

    other = (me + spots) % ctx_count
    half = spots // 2
    greet((me, place.owner(0, 2)))
    for away in (spots + half + 1, spots + half, spots + half - 1):
        greet((across(away), tp))
    for own in (0, 1):
        greet((other, place.owner(own, 2)))
    for step in (1, 3):
        greet((me, place.owner(0, step)))
    greet((me, place.owner(1, 2)))
    for away in range(1, ctx_count):
        if away not in (spots + half + 1, spots + half, spots + half - 1):
            greet((across(away), tp))
    for step in (1, 3):
        for own in (0, 1):
            greet((other, place.owner(own, step)))
    greet((other, place.owner(0, 0)))
    for step in (1, 3):
        greet((me, place.owner(1, step)))
    greet(place.far)

    pairs = ((act_hbm, act), (taps_hbm, taps), (blocks_hbm, blocks), (gains_hbm, gains),
             (forward_hbm, forward), (inverse_hbm, inverse), (twiddle_hbm, twiddle))
    inputs = [pltpu.make_async_copy(source, target, in_sems.at[k]) for k, (source, target) in enumerate(pairs)]
    inputs[0].start()
    fetch(0, lambda copy: copy.start())
    inputs[1].start()

    ahead = 6
    for t in range(1, ahead):
        fetch(t, lambda copy: copy.start())
    for copy in inputs[2:]:
        copy.start()

    def next_tile(t):
        fetch(t, lambda copy: copy.wait())
        if t + ahead < len(tiles):
            fetch(t + ahead, lambda copy: copy.start())

    inputs[0].wait()

    links = Links(send_sems, recv_sems)

    def over_crowd(src, dst):
        device = lambda peer: (peer // tp_count * spots + spot, peer % tp_count)
        return Swap(links, crowd, side * tp_count + tp, device, src, dst)

    def over_side(src, dst):
        return Swap(links, spots, spot, lambda peer: (side * spots + peer, tp), src, dst)

    def over_ctx(src, dst):
        return Swap(links, ctx_count, me, lambda peer: (peer, tp), src, dst)

    def span(index, size):
        return pl.ds(pl.multiple_of(index * size, size), size)

    tap_swap = over_crowd(
        lambda peer: taps_out.at[:, span(peer % tp_count * SIDES + peer // tp_count, piece)], lambda mine: taps_in.at[mine]
    )
    filt_swap = over_side(lambda peer: taps_t.at[:, span(peer, lanes)], lambda mine: filt_in.at[mine])
    gated_swap, conv_swap, home_swap = [], [], []
    for c in range(SETS):
        gated_swap.append(over_ctx(lambda peer, c=c: gated_t.at[c, span(peer, lanes)], lambda mine, c=c: gated_in.at[c, mine]))
        conv_swap.append(over_side(lambda peer, c=c: conv_out.at[c, peer], lambda mine, c=c: conv_in.at[c, span(mine, lanes)]))
        home_swap.append(over_crowd(lambda peer, c=c: conv_home.at[c, span(peer, out_tokens)], lambda mine, c=c: conv_final.at[c, mine]))

    def send_taps():
        inputs[1].wait()
        taps_out[...] = taps[...].astype(BF)
        tap_swap.start()

    def kv_part(c):
        def part(owner, which, half):
            rows = pl.ds(0, ROWS_Z) if which == 0 else pl.ds(ROWS_Z, tokens - ROWS_Z)
            return kv.at[owner, rows, pl.ds((2 * c + half) * piece, piece)]
        return part

    z_half, x_half = LANES_Z // 2, (channels - LANES_Z) // 2

    def q_part(owner, which, half):
        return qs.at[owner, :, pl.ds(half * z_half, z_half) if which == 0 else pl.ds(LANES_Z + half * x_half, x_half)]

    spreads = (
        Spread(place, links, kv_part(0), (a_z1, a_z2, a_zx, a_x1, a_x2, a_x3)),
        Spread(place, links, kv_part(1), (b_z1, b_z2, b_zx, b_x1, b_x2, b_x3)),
        Spread(place, links, q_part, (q_z1, q_z2, q_zx, q_x1, q_x2, q_x3)),
    )

    def multiply_kv(own, step, c):
        t = order.index((own, step, c))
        next_tile(t)
        block = jnp.dot(act[...], wbuf[t], preferred_element_type=F32)
        kv[place.owner(own, step), :, pl.ds(c * tile, tile)] = block.astype(BF)

    def multiply_q(t):
        next_tile(len(order) + t)
        block = jnp.dot(act[...], wbuf[len(order) + t], preferred_element_type=F32).astype(BF)
        qs[:, :, pl.ds(t * tile, tile)] = block.reshape(tp_count, out_tokens, tile)

    def mask():
        for copy in inputs[2:]:
            copy.wait()
        tap_swap.wait_recv()
        taps_in[side * tp_count + tp] = taps_out[:, span(tp * SIDES + side, piece)]
        for c in range(SETS):
            at = span((tp * SIDES + side) * SETS + c, part)
            depth_of = blocks[at].reshape(1, part)
            gain_t[c] = jnp.broadcast_to(gains[at].reshape(1, part), (part, part)).T
            for n in range(crowd * out_tokens // INNER):
                per = INNER // out_tokens
                block = taps_in[pl.ds(n * per, per), :, pl.ds(c * part, part)].reshape(INNER, part).astype(F32)
                index = n * INNER // tokens * spots + spot
                taps_t[c, :, pl.ds(n * INNER, INNER)] = jnp.where(index < depth_of, block, 0.0).T.astype(BF)
        filt_swap.start()

    rows = staged.shape[1] // 2

    fold = tokens // INNER

    def filter_spectrum():
        filt_swap.wait_recv()
        filt_in[spot] = taps_t[:, span(spot, lanes), :]
        for c in range(SETS):
            parts = []
            for a in range(OUTER):
                i, u = a // fold, a % fold
                parts.append(filt_in[i % spots, c, :, pl.ds((i // spots * fold + u) * INNER, INNER)])
            spectrum(parts, staged.at[c], twiddle)
            for n in range(2):
                at = pl.ds(n * rows, rows)
                filt_spec[c, at, :] = both(staged[c, at, :], forward)

    def finish(c):
        spreads[c].finish()
        if c < SETS:
            for which, at in ((0, pl.ds(0, ROWS_Z)), (1, pl.ds(ROWS_Z, tokens - ROWS_Z))):
                gated[at, pl.ds(c * piece, piece)] = spreads[c].total(which, 0) * spreads[c].total(which, 1)

    def gate(c):
        transposed(gated.at[:, pl.ds(c * piece, piece)], gated_t.at[c], tokens, piece)
        gated_swap[c].start()

    def convolve(c):
        gated_swap[c].wait_recv()
        gated_in[c, me] = gated_t[c, span(me, lanes), :]
        parts = [gated_in[c, a // fold, :, pl.ds(a % fold * INNER, INNER)] for a in range(OUTER)]
        spectrum(parts, staged.at[c], twiddle)
        for n in range(2):
            at = pl.ds(n * rows, rows)
            a, b = both(staged[c, at, :], forward), filt_spec[c, at, :]
            a_re, a_im, b_re, b_im = a[:, :INNER], a[:, INNER:], b[:, :INNER], b[:, INNER:]
            prod = jnp.concatenate([a_re * b_re - a_im * b_im, a_re * b_im + a_im * b_re], axis=1)
            mixed[at, :] = both(prod.astype(BF), inverse)
        data = []
        for f in range(OUTER):
            cos, sin = twiddle[0, pl.ds(f, 1), :], twiddle[1, pl.ds(f, 1), :]
            row = pl.ds(f * lanes, lanes)
            re, im = mixed[row, pl.ds(0, INNER)], mixed[row, pl.ds(INNER, INNER)]
            data.append((re * cos - im * sin, re * sin + im * cos))
        gain = gain_t[c, span(spot, lanes), :]
        for a, block in enumerate(outer_inverse(data)):
            i, u = a // fold, a % fold
            at = pl.ds((i // spots * fold + u) * INNER, INNER)
            conv_out[c, i % spots, :, at] = (block + gain * parts[a].astype(F32)).astype(BF)
        conv_swap[c].start()

    def home(c):
        conv_swap[c].wait_recv()
        conv_in[c, span(spot, lanes), :] = conv_out[c, spot]
        transposed(conv_in.at[c], conv_home.at[c], part, SIDES * tokens)
        home_swap[c].start()

    def finale():
        query = jnp.concatenate([spreads[SETS].total(which, half) for which in (0, 1) for half in (0, 1)], axis=1)
        for c in [step[1] for step in SCHEDULE if step[0] == "home"]:
            home_swap[c].wait_recv()
            conv_final[c, side * tp_count + tp] = conv_home[c, span(side * tp_count + tp, out_tokens), :]
            for peer in range(crowd):
                first = ((peer % tp_count * SIDES + peer // tp_count) * SETS + c) * part
                at = slice(first, first + part)
                out[:, at] = (query[:, at] * conv_final[c, peer].astype(F32)).astype(BF)

    steps = {
        "bar": lambda: pl.semaphore_wait(barrier, 2 * tp_count + ctx_count - 3),
        "mm": multiply_kv,
        "mq": multiply_q,
        "tap": send_taps,
        "mask": mask,
        "filt": filter_spectrum,
        "z1": lambda c, own: spreads[c].start_z1(own),
        "x1": lambda c, step: spreads[c].start_x1(step),
        "z2f": lambda c, own, way: spreads[c].start_z2_free(own, way),
        "pz1": lambda c, own, way: spreads[c].pass_z1(own, way),
        "tx1": lambda c, step: spreads[c].take_x1(step),
        "x2": lambda c: spreads[c].start_x2(),
        "x3f": lambda c, way: spreads[c].start_x3_free(way),
        "px2": lambda c, way: spreads[c].pass_x2(way),
        "zx": lambda c, half: spreads[c].start_zx(half),
        "fin": finish,
        "gate": gate,
        "conv": convolve,
        "home": home,
        "out": finale,
        "drain": links.drain,
    }
    for step in SCHEDULE:
        steps[step[0]](*step[1:])

    links.drain(len(links.started))


def on_device(activations, proj_weight, filter_taps, filter_blocks, skip_gain):
    tokens, depth_here = activations.shape
    channels, out_tokens = filter_taps.shape
    tp_count, ctx_count = lax.axis_size("tp"), lax.axis_size("ctx")
    depth = 4
    width = channels // tp_count
    forward, inverse, twiddle = tables()

    def buffers(z_rows, z_lanes, x_rows, x_lanes):
        return [
            pltpu.VMEM((2, 2, z_rows, z_lanes), BF),
            pltpu.VMEM((2, 2, 2, z_rows, z_lanes), BF),
            pltpu.VMEM((2, z_rows, z_lanes), BF),
            pltpu.VMEM((4, 2, x_rows, x_lanes), BF),
            pltpu.VMEM((2, x_rows, x_lanes), BF),
            pltpu.VMEM((2, 2, x_rows, x_lanes), BF),
        ]

    tile = width
    n_tiles = 3 * channels // tile
    n_copies = (SETS + 1) * 28 + (1 + SETS) * (2 * tp_count + ctx_count // SIDES - 2) + SETS * (ctx_count - 1)
    piece = width // SETS
    lanes = piece // ctx_count
    spots = ctx_count // SIDES
    part = lanes * spots
    crowd = SIDES * tp_count
    spec_rows = OUTER * lanes
    scratch = (
        [
            pltpu.VMEM((tokens, depth_here), BF),
            pltpu.VMEM((out_tokens, channels), F32),
            pltpu.VMEM((channels,), jnp.int32),
            pltpu.VMEM((channels,), F32),
            pltpu.VMEM(forward.shape, BF),
            pltpu.VMEM(inverse.shape, BF),
            pltpu.VMEM(twiddle.shape, F32),
            pltpu.VMEM((n_tiles, depth_here, tile), BF),
            pltpu.VMEM((tp_count, tokens, 2 * width), BF),
            pltpu.VMEM((tp_count, out_tokens, channels), BF),
        ]
        + buffers(ROWS_Z, piece, tokens - ROWS_Z, piece)
        + buffers(ROWS_Z, piece, tokens - ROWS_Z, piece)
        + buffers(out_tokens, LANES_Z // 2, out_tokens, (channels - LANES_Z) // 2)
        + [
            pltpu.VMEM((out_tokens, channels), BF),
            pltpu.VMEM((crowd, out_tokens, piece), BF),
            pltpu.VMEM((SETS, part, SIDES * tokens), BF),
            pltpu.VMEM((spots, SETS, lanes, SIDES * tokens), BF),
            pltpu.VMEM((SETS, spec_rows, 2 * INNER), BF),
            pltpu.VMEM((SETS, spec_rows, 2 * INNER), F32),
            pltpu.VMEM((SETS, part, part), F32),
            pltpu.VMEM((tokens, width), F32),
            pltpu.VMEM((SETS, piece, tokens), BF),
            pltpu.VMEM((SETS, ctx_count, lanes, tokens), BF),
            pltpu.VMEM((spec_rows, 2 * INNER), F32),
            pltpu.VMEM((SETS, spots, lanes, SIDES * tokens), BF),
            pltpu.VMEM((SETS, part, SIDES * tokens), BF),
            pltpu.VMEM((SETS, SIDES * tokens, part), BF),
            pltpu.VMEM((SETS, crowd, out_tokens, part), BF),
            pltpu.SemaphoreType.DMA((4 * n_tiles,)),
            pltpu.SemaphoreType.DMA((7,)),
            pltpu.SemaphoreType.DMA((n_copies,)),
            pltpu.SemaphoreType.DMA((n_copies,)),
        ]
    )
    vmem = pl.BlockSpec(memory_space=pltpu.VMEM)
    out = pl.pallas_call(
        functools.partial(kernel, depth=depth, tp_count=tp_count, ctx_count=ctx_count),
        out_shape=pltpu.VMEM((out_tokens, channels), BF),
        in_specs=[pl.BlockSpec(memory_space=pl.ANY)] * 8,
        out_specs=vmem,
        scratch_shapes=scratch,
        compiler_params=pltpu.CompilerParams(collective_id=0, has_side_effects=True, vmem_limit_bytes=60 * 2**20),
        name="hyena",
    )(
        activations,
        proj_weight,
        filter_taps.T,
        filter_blocks,
        skip_gain,
        jnp.asarray(forward),
        jnp.asarray(inverse),
        jnp.asarray(twiddle),
    )
    return out.T


def solution(mesh):
    placed = (P("ctx", "tp"), P("tp", None), P(None, ("ctx", "tp")), P(), P())
    return jax.shard_map(
        on_device, mesh=mesh, in_specs=placed, out_specs=P(None, ("ctx", "tp")), check_vma=False
    )
```

```python
import functools
import math

import jax
import jax.numpy as jnp
import ml_dtypes
import numpy as np
from jax import lax
from jax.experimental import pallas as pl
from jax.experimental.pallas import tpu as pltpu
from jax.sharding import PartitionSpec as P

BF = jnp.bfloat16
F32 = jnp.float32
OUTER = 32
INNER = 128
LENGTH = OUTER * INNER
SIDES = 2
SETS = 2
SHIFT = 0.25

ROWS_Z = 160
LANES_Z = 2560

SCHEDULE = (
    ("mm", 0, 3, 0), ("mm", 1, 2, 1), ("mm", 0, 2, 0), ("bar",), ("tap",), ("mm", 0, 3, 1), ("mm", 0, 2, 1), ("z1", 1, 1),
    ("mm", 0, 0, 1), ("x1", 0, 3), ("mm", 1, 2, 0), ("z1", 0, 0), ("x1", 1, 0), ("z2f", 0, 0, 1), ("mm", 0, 1, 0), ("z1", 1, 0),
    ("mm", 0, 0, 0), ("mm", 0, 1, 1), ("x1", 0, 2), ("mm", 1, 3, 0), ("z2f", 1, 0, 0), ("z2f", 1, 0, 1), ("x1", 1, 2),
    ("mm", 1, 0, 0), ("z1", 0, 1), ("mm", 1, 1, 0), ("mask",), ("x1", 0, 1), ("z2f", 0, 0, 0), ("mm", 1, 0, 1), ("x1", 1, 3),
    ("mm", 1, 3, 1), ("drain", 7), ("pz1", 0, 0, 1), ("pz1", 1, 0, 0), ("tx1", 0, 3), ("x3f", 0, 1), ("x1", 1, 1),
    ("mm", 1, 1, 1), ("x1", 0, 0), ("pz1", 1, 1, 1), ("pz1", 0, 0, 0), ("mq", 0), ("tx1", 0, 2), ("x2", 0), ("mq", 1),
    ("drain", 18), ("tx1", 1, 2), ("x2", 1), ("pz1", 1, 1, 0), ("drain", 24), ("tx1", 0, 1), ("pz1", 1, 0, 1), ("mq", 2),
    ("pz1", 0, 1, 0), ("drain", 29), ("zx", 0, 0), ("z2f", 0, 1, 0), ("mq", 3), ("mq", 4), ("zx", 1, 0), ("mq", 5),
    ("pz1", 0, 1, 1), ("zx", 0, 1), ("tx1", 1, 3), ("z2f", 0, 1, 1), ("filt",), ("z2f", 1, 1, 0), ("mq", 6), ("tx1", 1, 1),
    ("x3f", 0, 0), ("px2", 0, 0), ("px2", 0, 1), ("px2", 1, 1), ("zx", 1, 1), ("mq", 7), ("px2", 1, 0), ("x1", 2, 3),
    ("x3f", 1, 1), ("z2f", 1, 1, 1), ("x1", 2, 2), ("x3f", 1, 0), ("z1", 2, 0), ("z1", 2, 1), ("z2f", 2, 0, 0), ("z2f", 2, 0, 1),
    ("drain", 54), ("fin", 0), ("gate", 0), ("drain", 59), ("fin", 1), ("gate", 1), ("x1", 2, 1), ("pz1", 2, 0, 1), ("x1", 2, 0),
    ("z2f", 2, 1, 1), ("tx1", 2, 2), ("pz1", 2, 0, 0), ("x2", 2), ("tx1", 2, 3), ("drain", 66), ("pz1", 2, 1, 0),
    ("z2f", 2, 1, 0), ("conv", 0), ("drain", 70), ("conv", 1), ("zx", 2, 1), ("x3f", 2, 1), ("tx1", 2, 1), ("x3f", 2, 0),
    ("zx", 2, 0), ("pz1", 2, 1, 1), ("drain", 80), ("home", 0), ("px2", 2, 0), ("px2", 2, 1), ("drain", 86), ("home", 1),
    ("drain", 91), ("fin", 2), ("out",),
)


def flipped(index):
    return int(format(index, "05b")[::-1], 2)


def tables():
    at = np.arange(INNER)
    angle = 2.0 * math.pi * (at[:, None] * at[None, :] % INNER) / INNER
    cos, sin = np.cos(angle), np.sin(angle)
    forward = np.block([[cos, -sin], [sin, cos]])
    inverse = np.block([[cos, sin], [-sin, cos]])
    freqs = np.array([flipped(f) for f in range(OUTER)]) + SHIFT
    turn = 2.0 * math.pi * freqs[:, None] * at[None, :] / LENGTH

    def halves(matrix):
        high = matrix.astype(ml_dtypes.bfloat16)
        low = (matrix - high.astype(np.float64)).astype(ml_dtypes.bfloat16)
        return np.stack([high, low])

    twiddle = np.stack([np.cos(turn), np.sin(turn)]).astype(np.float32)
    return halves(forward), halves(inverse / LENGTH), twiddle


def times(pair, turn):
    re, im = pair
    turn = turn % 1.0
    if turn == 0.0:
        return pair
    if turn == 0.25:
        return (-im, re)
    if turn == 0.5:
        return (-re, -im)
    if turn == 0.75:
        return (im, -re)
    c, s = math.cos(2 * math.pi * turn), math.sin(2 * math.pi * turn)
    return (re * c - im * s, re * s + im * c)


def outer_forward(blocks):
    data = []
    for a, block in enumerate(blocks):
        angle = -2.0 * math.pi * a * SHIFT / OUTER
        data.append((block * math.cos(angle), block * math.sin(angle)) if a else (block, jnp.zeros_like(block)))
    half = OUTER // 2
    while half >= 1:
        for start in range(0, OUTER, 2 * half):
            for k in range(half):
                a, b = data[start + k], data[start + k + half]
                data[start + k] = (a[0] + b[0], a[1] + b[1])
                data[start + k + half] = times((a[0] - b[0], a[1] - b[1]), -k / (2 * half))
        half //= 2
    return data


def outer_inverse(data):
    data = list(data)
    half = 1
    while half < OUTER:
        for start in range(0, OUTER, 2 * half):
            for k in range(half):
                a, b = data[start + k], times(data[start + k + half], k / (2 * half))
                data[start + k] = (a[0] + b[0], a[1] + b[1])
                data[start + k + half] = (a[0] - b[0], a[1] - b[1])
        half *= 2
    out = []
    for a, (re, im) in enumerate(data):
        angle = 2.0 * math.pi * a * SHIFT / OUTER
        out.append(re * math.cos(angle) - im * math.sin(angle))
    return out


class Spread:
    def __init__(self, place, links, part, bufs):
        self.place, self.links, self.part = place, links, part
        self.z1, self.z2, self.zx, self.x1, self.x2, self.x3 = bufs
        self.pending = {}

    def cell(self, own, step, piece, half):
        return self.part(self.place.owner(own, step), piece, half)

    def send(self, key, src, dst, to):
        self.pending[key] = self.links.send(src, dst, to)

    def start_z1(self, own):
        for way in (0, 1):
            self.send(("z1", own, way), self.cell(own, 2, 0, way), self.z1.at[way, own], self.place.zway[way])

    def start_x1(self, step):
        for half in (0, 1):
            self.send(("x1", step, half), self.cell(0, step, 1, half), self.x1.at[step, half], self.place.far)

    def start_z2_free(self, own, way):
        step = (1, 3)[way]
        self.send(("z2", own, way, 1 - way), self.cell(own, step, 0, 1 - way), self.z2.at[way, own, 1 - way], self.place.zway[way])

    def pass_z1(self, own, way):
        self.pending[("z1", own, way)].wait_recv()
        cell = self.cell(own, (1, 3)[way], 0, way)
        cell[...] = (cell[...].astype(F32) + self.z1[way, own].astype(F32)).astype(BF)
        self.send(("z2", own, way, way), cell, self.z2.at[way, own, way], self.place.zway[way])

    def take_x1(self, step):
        for half in (0, 1):
            self.pending[("x1", step, half)].wait_recv()
            cell = self.cell(1, step, 1, half)
            cell[...] = (cell[...].astype(F32) + self.x1[step, half].astype(F32)).astype(BF)

    def start_x2(self):
        for way in (0, 1):
            self.send(("x2", way), self.cell(1, 2, 1, way), self.x2.at[way], self.place.zway[way])

    def start_x3_free(self, way):
        self.send(("x3", way, 1 - way), self.cell(1, (1, 3)[way], 1, 1 - way), self.x3.at[way, 1 - way], self.place.zway[way])

    def pass_x2(self, way):
        self.pending[("x2", way)].wait_recv()
        cell = self.cell(1, (1, 3)[way], 1, way)
        cell[...] = (cell[...].astype(F32) + self.x2[way].astype(F32)).astype(BF)
        self.send(("x3", way, way), cell, self.x3.at[way, way], self.place.zway[way])

    def start_zx(self, half):
        for way in (0, 1):
            self.pending[("z2", 0, way, half)].wait_recv()
        cell = self.cell(0, 0, 0, half)
        total = cell[...].astype(F32) + self.z2[0, 0, half].astype(F32) + self.z2[1, 0, half].astype(F32)
        cell[...] = total.astype(BF)
        self.send(("zx", half), cell, self.zx.at[half], self.place.far)

    def finish(self):
        for half in (0, 1):
            self.pending[("x1", 0, half)].wait_recv()
            for way in (0, 1):
                self.pending[("z2", 1, way, half)].wait_recv()
                self.pending[("x3", way, half)].wait_recv()
            self.pending[("zx", half)].wait_recv()

    def total(self, piece, half):
        mine = self.cell(1, 0, piece, half)[...].astype(F32)
        if piece == 0:
            terms = (self.z2[0, 1, half], self.z2[1, 1, half], self.zx[half])
        else:
            terms = (self.x1[0, half], self.x3[0, half], self.x3[1, half])
        for term in terms:
            mine = mine + term.astype(F32)
        return mine


class Place:
    def __init__(self, depth, tp_count, ctx_count):
        self.ctx, self.tp = lax.axis_index("ctx"), lax.axis_index("tp")
        self.depth, self.tp_count, self.ctx_count = depth, tp_count, ctx_count
        self.x_half, self.z = self.tp // depth, self.tp % depth
        self.zway = tuple((self.ctx, self.x_half * depth + (self.z + step) % depth) for step in (1, depth - 1))
        self.far = (self.ctx, (self.tp + depth) % tp_count)

    def owner(self, own, step):
        half = self.x_half if own else 1 - self.x_half
        return half * self.depth + (self.z + step) % self.depth


class Links:
    def __init__(self, send_sems, recv_sems):
        self.send_sems, self.recv_sems = send_sems, recv_sems
        self.used = 0
        self.drained = 0
        self.started = []

    def make(self, src, dst, to, at):
        return pltpu.make_async_remote_copy(
            src_ref=src,
            dst_ref=dst,
            send_sem=self.send_sems.at[at],
            recv_sem=self.recv_sems.at[at],
            device_id=to,
            device_id_type=pl.DeviceIdType.MESH,
        )

    def send(self, src, dst, to):
        copy = self.make(src, dst, to, self.used)
        self.used += 1
        copy.start()
        self.started.append(copy)
        return copy

    def drain(self, count):
        for at in range(self.drained, count):
            self.started[at].wait_send()
        self.drained = max(self.drained, count)


class Swap:
    def __init__(self, links, count, me, device, src, dst):
        self.links, self.count, self.me, self.device, self.src, self.dst = links, count, me, device, src, dst
        self.base = links.used
        links.used += count - 1

    def copy(self, away):
        peer = (self.me + away) % self.count
        return self.links.make(self.src(peer), self.dst(self.me), self.device(peer), self.base + away - 1)

    def each(self, act):
        lax.fori_loop(1, self.count, lambda away, carry: (act(self.copy(away)), carry)[1], 0)

    def start(self):
        self.each(lambda copy: copy.start())
        self.links.started.append(self)

    def wait_recv(self):
        self.each(lambda copy: copy.wait_recv())

    def wait_send(self):
        self.each(lambda copy: copy.wait_send())


def transposed(source, target, rows, lanes):
    for r in range(0, rows, 128):
        for c in range(0, lanes, 128):
            tile = source[pl.ds(r, 128), pl.ds(c, 128)].astype(F32)
            target[pl.ds(c, 128), pl.ds(r, 128)] = tile.T.astype(target.dtype)


def spectrum(blocks, staged, twiddle):
    lanes = blocks[0].shape[0]
    for f, (re, im) in enumerate(outer_forward([block.astype(F32) for block in blocks])):
        c, s = twiddle[0, pl.ds(f, 1), :], twiddle[1, pl.ds(f, 1), :]
        staged[pl.ds(f * lanes, lanes), pl.ds(0, INNER)] = (re * c + im * s).astype(BF)
        staged[pl.ds(f * lanes, lanes), pl.ds(INNER, INNER)] = (im * c - re * s).astype(BF)


def both(data, matrix):
    return jnp.dot(data, matrix[0], preferred_element_type=F32) + jnp.dot(data, matrix[1], preferred_element_type=F32)


def kernel(
    act_hbm, weight, taps_hbm, blocks_hbm, gains_hbm, forward_hbm, inverse_hbm, twiddle_hbm,
    out,
    act, taps, blocks, gains, forward, inverse, twiddle,
    wbuf, kv, qs,
    a_z1, a_z2, a_zx, a_x1, a_x2, a_x3,
    b_z1, b_z2, b_zx, b_x1, b_x2, b_x3,
    q_z1, q_z2, q_zx, q_x1, q_x2, q_x3,
    taps_out, taps_in, taps_t, filt_in, staged, filt_spec, gain_t,
    gated, gated_t, gated_in, mixed, conv_out, conv_in, conv_home, conv_final,
    w_sems, in_sems, send_sems, recv_sems,
    *, depth, tp_count, ctx_count,
):
    place = Place(depth, tp_count, ctx_count)
    me, tp = place.ctx, place.tp
    tokens, width = gated.shape
    out_tokens = tokens // tp_count
    channels = tp_count * width
    tile = wbuf.shape[2]
    piece = width // SETS
    lanes = piece // ctx_count
    spots = ctx_count // SIDES
    part = lanes * spots
    side, spot = me // spots, me % spots
    crowd = SIDES * tp_count

    order = [step[1:] for step in SCHEDULE if step[0] == "mm"]
    tiles = []
    for own, step, c in order:
        base = place.owner(own, step) * width + c * part
        tiles.append([(which * channels + base + side * piece, part) for which in (1, 2) for side in range(SIDES)])
    for t in range(channels // tile):
        tiles.append([(t * tile, tile)])

    def fetch(t, act_on):
        at = 0
        for k, (column, size) in enumerate(tiles[t]):
            src = weight.at[:, pl.ds(pl.multiple_of(column, size), size)]
            act_on(pltpu.make_async_copy(src, wbuf.at[t, :, pl.ds(at, size)], w_sems.at[4 * t + k]))
            at += size

    barrier = pltpu.get_barrier_semaphore()

    def greet(device):
        pl.semaphore_signal(barrier, inc=1, device_id=device, device_id_type=pl.DeviceIdType.MESH)

    def across(away):
        return (me + away) % ctx_count

    other = (me + spots) % ctx_count
    half = spots // 2
    greet((me, place.owner(0, 2)))
    for away in (spots + half + 1, spots + half, spots + half - 1):
        greet((across(away), tp))
    for own in (0, 1):
        greet((other, place.owner(own, 2)))
    for step in (1, 3):
        greet((me, place.owner(0, step)))
    greet((me, place.owner(1, 2)))
    for away in range(1, ctx_count):
        if away not in (spots + half + 1, spots + half, spots + half - 1):
            greet((across(away), tp))
    for step in (1, 3):
        for own in (0, 1):
            greet((other, place.owner(own, step)))
    greet((other, place.owner(0, 0)))
    for step in (1, 3):
        greet((me, place.owner(1, step)))
    greet(place.far)

    pairs = ((act_hbm, act), (taps_hbm, taps), (blocks_hbm, blocks), (gains_hbm, gains),
             (forward_hbm, forward), (inverse_hbm, inverse), (twiddle_hbm, twiddle))
    inputs = [pltpu.make_async_copy(source, target, in_sems.at[k]) for k, (source, target) in enumerate(pairs)]
    inputs[0].start()
    fetch(0, lambda copy: copy.start())

    ahead = 4
    for t in range(1, ahead):
        fetch(t, lambda copy: copy.start())
    for copy in inputs[1:]:
        copy.start()

    def next_tile(t):
        fetch(t, lambda copy: copy.wait())
        if t + ahead < len(tiles):
            fetch(t + ahead, lambda copy: copy.start())

    inputs[0].wait()

    links = Links(send_sems, recv_sems)

    def over_crowd(src, dst):
        device = lambda peer: (peer // tp_count * spots + spot, peer % tp_count)
        return Swap(links, crowd, side * tp_count + tp, device, src, dst)

    def over_side(src, dst):
        return Swap(links, spots, spot, lambda peer: (side * spots + peer, tp), src, dst)

    def over_ctx(src, dst):
        return Swap(links, ctx_count, me, lambda peer: (peer, tp), src, dst)

    def span(index, size):
        return pl.ds(pl.multiple_of(index * size, size), size)

    tap_swap = over_crowd(
        lambda peer: taps_out.at[:, span(peer % tp_count * SIDES + peer // tp_count, piece)], lambda mine: taps_in.at[mine]
    )
    filt_swap = over_side(lambda peer: taps_t.at[:, span(peer, lanes)], lambda mine: filt_in.at[mine])
    gated_swap, conv_swap, home_swap = [], [], []
    for c in range(SETS):
        gated_swap.append(over_ctx(lambda peer, c=c: gated_t.at[c, span(peer, lanes)], lambda mine, c=c: gated_in.at[c, mine]))
        conv_swap.append(over_side(lambda peer, c=c: conv_out.at[c, peer], lambda mine, c=c: conv_in.at[c, span(mine, lanes)]))
        home_swap.append(over_crowd(lambda peer, c=c: conv_home.at[c, span(peer, out_tokens)], lambda mine, c=c: conv_final.at[c, mine]))

    def send_taps():
        inputs[1].wait()
        taps_out[...] = taps[...].astype(BF)
        tap_swap.start()

    def kv_part(c):
        def part(owner, which, half):
            rows = pl.ds(0, ROWS_Z) if which == 0 else pl.ds(ROWS_Z, tokens - ROWS_Z)
            return kv.at[owner, rows, pl.ds((2 * c + half) * piece, piece)]
        return part

    z_half, x_half = LANES_Z // 2, (channels - LANES_Z) // 2

    def q_part(owner, which, half):
        return qs.at[owner, :, pl.ds(half * z_half, z_half) if which == 0 else pl.ds(LANES_Z + half * x_half, x_half)]

    spreads = (
        Spread(place, links, kv_part(0), (a_z1, a_z2, a_zx, a_x1, a_x2, a_x3)),
        Spread(place, links, kv_part(1), (b_z1, b_z2, b_zx, b_x1, b_x2, b_x3)),
        Spread(place, links, q_part, (q_z1, q_z2, q_zx, q_x1, q_x2, q_x3)),
    )

    def multiply_kv(own, step, c):
        t = order.index((own, step, c))
        next_tile(t)
        block = jnp.dot(act[...], wbuf[t], preferred_element_type=F32)
        kv[place.owner(own, step), :, pl.ds(c * tile, tile)] = block.astype(BF)

    def multiply_q(t):
        next_tile(len(order) + t)
        block = jnp.dot(act[...], wbuf[len(order) + t], preferred_element_type=F32).astype(BF)
        qs[:, :, pl.ds(t * tile, tile)] = block.reshape(tp_count, out_tokens, tile)

    def mask():
        for copy in inputs[2:]:
            copy.wait()
        tap_swap.wait_recv()
        taps_in[side * tp_count + tp] = taps_out[:, span(tp * SIDES + side, piece)]
        for c in range(SETS):
            at = span((tp * SIDES + side) * SETS + c, part)
            depth_of = blocks[at].reshape(1, part)
            gain_t[c] = jnp.broadcast_to(gains[at].reshape(1, part), (part, part)).T
            for n in range(crowd * out_tokens // INNER):
                per = INNER // out_tokens
                block = taps_in[pl.ds(n * per, per), :, pl.ds(c * part, part)].reshape(INNER, part).astype(F32)
                index = n * INNER // tokens * spots + spot
                taps_t[c, :, pl.ds(n * INNER, INNER)] = jnp.where(index < depth_of, block, 0.0).T.astype(BF)
        filt_swap.start()

    rows = staged.shape[1] // 2

    fold = tokens // INNER

    def filter_spectrum():
        filt_swap.wait_recv()
        filt_in[spot] = taps_t[:, span(spot, lanes), :]
        for c in range(SETS):
            parts = []
            for a in range(OUTER):
                i, u = a // fold, a % fold
                parts.append(filt_in[i % spots, c, :, pl.ds((i // spots * fold + u) * INNER, INNER)])
            spectrum(parts, staged.at[c], twiddle)
            for n in range(2):
                at = pl.ds(n * rows, rows)
                filt_spec[c, at, :] = both(staged[c, at, :], forward)

    def finish(c):
        spreads[c].finish()
        if c < SETS:
            for which, at in ((0, pl.ds(0, ROWS_Z)), (1, pl.ds(ROWS_Z, tokens - ROWS_Z))):
                gated[at, pl.ds(c * piece, piece)] = spreads[c].total(which, 0) * spreads[c].total(which, 1)

    def gate(c):
        transposed(gated.at[:, pl.ds(c * piece, piece)], gated_t.at[c], tokens, piece)
        gated_swap[c].start()

    def convolve(c):
        gated_swap[c].wait_recv()
        gated_in[c, me] = gated_t[c, span(me, lanes), :]
        parts = [gated_in[c, a // fold, :, pl.ds(a % fold * INNER, INNER)] for a in range(OUTER)]
        spectrum(parts, staged.at[c], twiddle)
        for n in range(2):
            at = pl.ds(n * rows, rows)
            a, b = both(staged[c, at, :], forward), filt_spec[c, at, :]
            a_re, a_im, b_re, b_im = a[:, :INNER], a[:, INNER:], b[:, :INNER], b[:, INNER:]
            prod = jnp.concatenate([a_re * b_re - a_im * b_im, a_re * b_im + a_im * b_re], axis=1)
            mixed[at, :] = both(prod.astype(BF), inverse)
        data = []
        for f in range(OUTER):
            cos, sin = twiddle[0, pl.ds(f, 1), :], twiddle[1, pl.ds(f, 1), :]
            row = pl.ds(f * lanes, lanes)
            re, im = mixed[row, pl.ds(0, INNER)], mixed[row, pl.ds(INNER, INNER)]
            data.append((re * cos - im * sin, re * sin + im * cos))
        gain = gain_t[c, span(spot, lanes), :]
        for a, block in enumerate(outer_inverse(data)):
            i, u = a // fold, a % fold
            at = pl.ds((i // spots * fold + u) * INNER, INNER)
            conv_out[c, i % spots, :, at] = (block + gain * parts[a].astype(F32)).astype(BF)
        conv_swap[c].start()

    def home(c):
        conv_swap[c].wait_recv()
        conv_in[c, span(spot, lanes), :] = conv_out[c, spot]
        transposed(conv_in.at[c], conv_home.at[c], part, SIDES * tokens)
        home_swap[c].start()

    def finale():
        query = jnp.concatenate([spreads[SETS].total(which, half) for which in (0, 1) for half in (0, 1)], axis=1)
        for c in [step[1] for step in SCHEDULE if step[0] == "home"]:
            home_swap[c].wait_recv()
            conv_final[c, side * tp_count + tp] = conv_home[c, span(side * tp_count + tp, out_tokens), :]
            for peer in range(crowd):
                first = ((peer % tp_count * SIDES + peer // tp_count) * SETS + c) * part
                at = slice(first, first + part)
                out[:, at] = (query[:, at] * conv_final[c, peer].astype(F32)).astype(BF)

    steps = {
        "bar": lambda: pl.semaphore_wait(barrier, 2 * tp_count + ctx_count - 3),
        "mm": multiply_kv,
        "mq": multiply_q,
        "tap": send_taps,
        "mask": mask,
        "filt": filter_spectrum,
        "z1": lambda c, own: spreads[c].start_z1(own),
        "x1": lambda c, step: spreads[c].start_x1(step),
        "z2f": lambda c, own, way: spreads[c].start_z2_free(own, way),
        "pz1": lambda c, own, way: spreads[c].pass_z1(own, way),
        "tx1": lambda c, step: spreads[c].take_x1(step),
        "x2": lambda c: spreads[c].start_x2(),
        "x3f": lambda c, way: spreads[c].start_x3_free(way),
        "px2": lambda c, way: spreads[c].pass_x2(way),
        "zx": lambda c, half: spreads[c].start_zx(half),
        "fin": finish,
        "gate": gate,
        "conv": convolve,
        "home": home,
        "out": finale,
        "drain": links.drain,
    }
    for step in SCHEDULE:
        steps[step[0]](*step[1:])

    links.drain(len(links.started))


def on_device(activations, proj_weight, filter_taps, filter_blocks, skip_gain):
    tokens, depth_here = activations.shape
    channels, out_tokens = filter_taps.shape
    tp_count, ctx_count = lax.axis_size("tp"), lax.axis_size("ctx")
    depth = 4
    width = channels // tp_count
    forward, inverse, twiddle = tables()

    def buffers(z_rows, z_lanes, x_rows, x_lanes):
        return [
            pltpu.VMEM((2, 2, z_rows, z_lanes), BF),
            pltpu.VMEM((2, 2, 2, z_rows, z_lanes), BF),
            pltpu.VMEM((2, z_rows, z_lanes), BF),
            pltpu.VMEM((4, 2, x_rows, x_lanes), BF),
            pltpu.VMEM((2, x_rows, x_lanes), BF),
            pltpu.VMEM((2, 2, x_rows, x_lanes), BF),
        ]

    tile = width
    n_tiles = 3 * channels // tile
    n_copies = (SETS + 1) * 28 + (1 + SETS) * (2 * tp_count + ctx_count // SIDES - 2) + SETS * (ctx_count - 1)
    piece = width // SETS
    lanes = piece // ctx_count
    spots = ctx_count // SIDES
    part = lanes * spots
    crowd = SIDES * tp_count
    spec_rows = OUTER * lanes
    scratch = (
        [
            pltpu.VMEM((tokens, depth_here), BF),
            pltpu.VMEM((out_tokens, channels), F32),
            pltpu.VMEM((channels,), jnp.int32),
            pltpu.VMEM((channels,), F32),
            pltpu.VMEM(forward.shape, BF),
            pltpu.VMEM(inverse.shape, BF),
            pltpu.VMEM(twiddle.shape, F32),
            pltpu.VMEM((n_tiles, depth_here, tile), BF),
            pltpu.VMEM((tp_count, tokens, 2 * width), BF),
            pltpu.VMEM((tp_count, out_tokens, channels), BF),
        ]
        + buffers(ROWS_Z, piece, tokens - ROWS_Z, piece)
        + buffers(ROWS_Z, piece, tokens - ROWS_Z, piece)
        + buffers(out_tokens, LANES_Z // 2, out_tokens, (channels - LANES_Z) // 2)
        + [
            pltpu.VMEM((out_tokens, channels), BF),
            pltpu.VMEM((crowd, out_tokens, piece), BF),
            pltpu.VMEM((SETS, part, SIDES * tokens), BF),
            pltpu.VMEM((spots, SETS, lanes, SIDES * tokens), BF),
            pltpu.VMEM((SETS, spec_rows, 2 * INNER), BF),
            pltpu.VMEM((SETS, spec_rows, 2 * INNER), F32),
            pltpu.VMEM((SETS, part, part), F32),
            pltpu.VMEM((tokens, width), F32),
            pltpu.VMEM((SETS, piece, tokens), BF),
            pltpu.VMEM((SETS, ctx_count, lanes, tokens), BF),
            pltpu.VMEM((spec_rows, 2 * INNER), F32),
            pltpu.VMEM((SETS, spots, lanes, SIDES * tokens), BF),
            pltpu.VMEM((SETS, part, SIDES * tokens), BF),
            pltpu.VMEM((SETS, SIDES * tokens, part), BF),
            pltpu.VMEM((SETS, crowd, out_tokens, part), BF),
            pltpu.SemaphoreType.DMA((4 * n_tiles,)),
            pltpu.SemaphoreType.DMA((7,)),
            pltpu.SemaphoreType.DMA((n_copies,)),
            pltpu.SemaphoreType.DMA((n_copies,)),
        ]
    )
    vmem = pl.BlockSpec(memory_space=pltpu.VMEM)
    out = pl.pallas_call(
        functools.partial(kernel, depth=depth, tp_count=tp_count, ctx_count=ctx_count),
        out_shape=pltpu.VMEM((out_tokens, channels), BF),
        in_specs=[pl.BlockSpec(memory_space=pl.ANY)] * 8,
        out_specs=vmem,
        scratch_shapes=scratch,
        compiler_params=pltpu.CompilerParams(collective_id=0, has_side_effects=True, vmem_limit_bytes=60 * 2**20),
        name="hyena",
    )(
        activations,
        proj_weight,
        filter_taps.T,
        filter_blocks,
        skip_gain,
        jnp.asarray(forward),
        jnp.asarray(inverse),
        jnp.asarray(twiddle),
    )
    return out.T


def solution(mesh):
    placed = (P("ctx", "tp"), P("tp", None), P(None, ("ctx", "tp")), P(), P())
    return jax.shard_map(
        on_device, mesh=mesh, in_specs=placed, out_specs=P(None, ("ctx", "tp")), check_vma=False
    )
```

```python
import functools
import math

import jax
import jax.numpy as jnp
import ml_dtypes
import numpy as np
from jax import lax
from jax.experimental import pallas as pl
from jax.experimental.pallas import tpu as pltpu
from jax.sharding import PartitionSpec as P

BF = jnp.bfloat16
F32 = jnp.float32
OUTER = 32
INNER = 128
LENGTH = OUTER * INNER
SIDES = 2
SETS = 2
SHIFT = 0.25

ROWS_Z = 160
LANES_Z = 2560

SCHEDULE = (
    ("mm", 0, 3, 0), ("mm", 1, 2, 1), ("mm", 0, 2, 0), ("bar",), ("tap",), ("mm", 0, 3, 1), ("mm", 0, 2, 1), ("z1", 1, 1),
    ("mm", 0, 0, 1), ("x1", 0, 3), ("mm", 1, 2, 0), ("z1", 0, 0), ("x1", 1, 0), ("z2f", 0, 0, 1), ("mm", 0, 1, 0), ("z1", 1, 0),
    ("mm", 0, 0, 0), ("mm", 0, 1, 1), ("x1", 0, 2), ("mm", 1, 3, 0), ("z2f", 1, 0, 0), ("z2f", 1, 0, 1), ("x1", 1, 2),
    ("mm", 1, 0, 0), ("z1", 0, 1), ("mm", 1, 1, 0), ("mask",), ("x1", 0, 1), ("z2f", 0, 0, 0), ("mm", 1, 0, 1), ("x1", 1, 3),
    ("mm", 1, 3, 1), ("drain", 7), ("pz1", 0, 0, 1), ("pz1", 1, 0, 0), ("tx1", 0, 3), ("x3f", 0, 1), ("x1", 1, 1),
    ("mm", 1, 1, 1), ("x1", 0, 0), ("pz1", 1, 1, 1), ("pz1", 0, 0, 0), ("mq", 0), ("tx1", 0, 2), ("x2", 0), ("mq", 1),
    ("drain", 18), ("tx1", 1, 2), ("x2", 1), ("pz1", 1, 1, 0), ("drain", 24), ("tx1", 0, 1), ("pz1", 1, 0, 1), ("mq", 2),
    ("pz1", 0, 1, 0), ("drain", 29), ("zx", 0, 0), ("z2f", 0, 1, 0), ("mq", 3), ("mq", 4), ("zx", 1, 0), ("mq", 5),
    ("pz1", 0, 1, 1), ("zx", 0, 1), ("tx1", 1, 3), ("z2f", 0, 1, 1), ("filt",), ("z2f", 1, 1, 0), ("mq", 6), ("tx1", 1, 1),
    ("x3f", 0, 0), ("px2", 0, 0), ("px2", 0, 1), ("px2", 1, 1), ("zx", 1, 1), ("mq", 7), ("px2", 1, 0), ("x1", 2, 3),
    ("x3f", 1, 1), ("z2f", 1, 1, 1), ("x1", 2, 2), ("x3f", 1, 0), ("z1", 2, 0), ("z1", 2, 1), ("z2f", 2, 0, 0), ("z2f", 2, 0, 1),
    ("drain", 54), ("fin", 0), ("gate", 0), ("drain", 59), ("fin", 1), ("gate", 1), ("x1", 2, 1), ("pz1", 2, 0, 1), ("x1", 2, 0),
    ("z2f", 2, 1, 1), ("tx1", 2, 2), ("pz1", 2, 0, 0), ("x2", 2), ("tx1", 2, 3), ("drain", 66), ("pz1", 2, 1, 0),
    ("z2f", 2, 1, 0), ("conv", 0), ("drain", 70), ("conv", 1), ("zx", 2, 1), ("x3f", 2, 1), ("tx1", 2, 1), ("x3f", 2, 0),
    ("zx", 2, 0), ("pz1", 2, 1, 1), ("drain", 80), ("home", 0), ("px2", 2, 0), ("px2", 2, 1), ("drain", 86), ("home", 1),
    ("drain", 91), ("fin", 2), ("out",),
)


def flipped(index):
    return int(format(index, "05b")[::-1], 2)


def tables():
    at = np.arange(INNER)
    angle = 2.0 * math.pi * (at[:, None] * at[None, :] % INNER) / INNER
    cos, sin = np.cos(angle), np.sin(angle)
    forward = np.block([[cos, -sin], [sin, cos]])
    inverse = np.block([[cos, sin], [-sin, cos]])
    freqs = np.array([flipped(f) for f in range(OUTER)]) + SHIFT
    turn = 2.0 * math.pi * freqs[:, None] * at[None, :] / LENGTH

    def halves(matrix):
        high = matrix.astype(ml_dtypes.bfloat16)
        low = (matrix - high.astype(np.float64)).astype(ml_dtypes.bfloat16)
        return np.stack([high, low])

    twiddle = np.stack([np.cos(turn), np.sin(turn)]).astype(np.float32)
    return halves(forward), halves(inverse / LENGTH), twiddle


def times(pair, turn):
    re, im = pair
    turn = turn % 1.0
    if turn == 0.0:
        return pair
    if turn == 0.25:
        return (-im, re)
    if turn == 0.5:
        return (-re, -im)
    if turn == 0.75:
        return (im, -re)
    c, s = math.cos(2 * math.pi * turn), math.sin(2 * math.pi * turn)
    return (re * c - im * s, re * s + im * c)


def outer_forward(blocks):
    data = []
    for a, block in enumerate(blocks):
        angle = -2.0 * math.pi * a * SHIFT / OUTER
        data.append((block * math.cos(angle), block * math.sin(angle)) if a else (block, jnp.zeros_like(block)))
    half = OUTER // 2
    while half >= 1:
        for start in range(0, OUTER, 2 * half):
            for k in range(half):
                a, b = data[start + k], data[start + k + half]
                data[start + k] = (a[0] + b[0], a[1] + b[1])
                data[start + k + half] = times((a[0] - b[0], a[1] - b[1]), -k / (2 * half))
        half //= 2
    return data


def outer_inverse(data):
    data = list(data)
    half = 1
    while half < OUTER:
        for start in range(0, OUTER, 2 * half):
            for k in range(half):
                a, b = data[start + k], times(data[start + k + half], k / (2 * half))
                data[start + k] = (a[0] + b[0], a[1] + b[1])
                data[start + k + half] = (a[0] - b[0], a[1] - b[1])
        half *= 2
    out = []
    for a, (re, im) in enumerate(data):
        angle = 2.0 * math.pi * a * SHIFT / OUTER
        out.append(re * math.cos(angle) - im * math.sin(angle))
    return out


class Spread:
    def __init__(self, place, links, part, bufs):
        self.place, self.links, self.part = place, links, part
        self.z1, self.z2, self.zx, self.x1, self.x2, self.x3 = bufs
        self.pending = {}

    def cell(self, own, step, piece, half):
        return self.part(self.place.owner(own, step), piece, half)

    def send(self, key, src, dst, to):
        self.pending[key] = self.links.send(src, dst, to)

    def start_z1(self, own):
        for way in (0, 1):
            self.send(("z1", own, way), self.cell(own, 2, 0, way), self.z1.at[way, own], self.place.zway[way])

    def start_x1(self, step):
        for half in (0, 1):
            self.send(("x1", step, half), self.cell(0, step, 1, half), self.x1.at[step, half], self.place.far)

    def start_z2_free(self, own, way):
        step = (1, 3)[way]
        self.send(("z2", own, way, 1 - way), self.cell(own, step, 0, 1 - way), self.z2.at[way, own, 1 - way], self.place.zway[way])

    def pass_z1(self, own, way):
        self.pending[("z1", own, way)].wait_recv()
        cell = self.cell(own, (1, 3)[way], 0, way)
        cell[...] = (cell[...].astype(F32) + self.z1[way, own].astype(F32)).astype(BF)
        self.send(("z2", own, way, way), cell, self.z2.at[way, own, way], self.place.zway[way])

    def take_x1(self, step):
        for half in (0, 1):
            self.pending[("x1", step, half)].wait_recv()
            cell = self.cell(1, step, 1, half)
            cell[...] = (cell[...].astype(F32) + self.x1[step, half].astype(F32)).astype(BF)

    def start_x2(self):
        for way in (0, 1):
            self.send(("x2", way), self.cell(1, 2, 1, way), self.x2.at[way], self.place.zway[way])

    def start_x3_free(self, way):
        self.send(("x3", way, 1 - way), self.cell(1, (1, 3)[way], 1, 1 - way), self.x3.at[way, 1 - way], self.place.zway[way])

    def pass_x2(self, way):
        self.pending[("x2", way)].wait_recv()
        cell = self.cell(1, (1, 3)[way], 1, way)
        cell[...] = (cell[...].astype(F32) + self.x2[way].astype(F32)).astype(BF)
        self.send(("x3", way, way), cell, self.x3.at[way, way], self.place.zway[way])

    def start_zx(self, half):
        for way in (0, 1):
            self.pending[("z2", 0, way, half)].wait_recv()
        cell = self.cell(0, 0, 0, half)
        total = cell[...].astype(F32) + self.z2[0, 0, half].astype(F32) + self.z2[1, 0, half].astype(F32)
        cell[...] = total.astype(BF)
        self.send(("zx", half), cell, self.zx.at[half], self.place.far)

    def finish(self):
        for half in (0, 1):
            self.pending[("x1", 0, half)].wait_recv()
            for way in (0, 1):
                self.pending[("z2", 1, way, half)].wait_recv()
                self.pending[("x3", way, half)].wait_recv()
            self.pending[("zx", half)].wait_recv()

    def total(self, piece, half):
        mine = self.cell(1, 0, piece, half)[...].astype(F32)
        if piece == 0:
            terms = (self.z2[0, 1, half], self.z2[1, 1, half], self.zx[half])
        else:
            terms = (self.x1[0, half], self.x3[0, half], self.x3[1, half])
        for term in terms:
            mine = mine + term.astype(F32)
        return mine


class Place:
    def __init__(self, depth, tp_count, ctx_count):
        self.ctx, self.tp = lax.axis_index("ctx"), lax.axis_index("tp")
        self.depth, self.tp_count, self.ctx_count = depth, tp_count, ctx_count
        self.x_half, self.z = self.tp // depth, self.tp % depth
        self.zway = tuple((self.ctx, self.x_half * depth + (self.z + step) % depth) for step in (1, depth - 1))
        self.far = (self.ctx, (self.tp + depth) % tp_count)

    def owner(self, own, step):
        half = self.x_half if own else 1 - self.x_half
        return half * self.depth + (self.z + step) % self.depth


class Links:
    def __init__(self, send_sems, recv_sems):
        self.send_sems, self.recv_sems = send_sems, recv_sems
        self.used = 0
        self.drained = 0
        self.started = []

    def make(self, src, dst, to, at):
        return pltpu.make_async_remote_copy(
            src_ref=src,
            dst_ref=dst,
            send_sem=self.send_sems.at[at],
            recv_sem=self.recv_sems.at[at],
            device_id=to,
            device_id_type=pl.DeviceIdType.MESH,
        )

    def send(self, src, dst, to):
        copy = self.make(src, dst, to, self.used)
        self.used += 1
        copy.start()
        self.started.append(copy)
        return copy

    def drain(self, count):
        for at in range(self.drained, count):
            self.started[at].wait_send()
        self.drained = max(self.drained, count)


class Swap:
    def __init__(self, links, count, me, device, src, dst):
        self.links, self.count, self.me, self.device, self.src, self.dst = links, count, me, device, src, dst
        self.base = links.used
        links.used += count - 1

    def copy(self, away):
        peer = (self.me + away) % self.count
        return self.links.make(self.src(peer), self.dst(self.me), self.device(peer), self.base + away - 1)

    def each(self, act):
        lax.fori_loop(1, self.count, lambda away, carry: (act(self.copy(away)), carry)[1], 0)

    def start(self):
        self.each(lambda copy: copy.start())
        self.links.started.append(self)

    def wait_recv(self):
        self.each(lambda copy: copy.wait_recv())

    def wait_send(self):
        self.each(lambda copy: copy.wait_send())


def transposed(source, target, rows, lanes):
    for r in range(0, rows, 128):
        for c in range(0, lanes, 128):
            tile = source[pl.ds(r, 128), pl.ds(c, 128)].astype(F32)
            target[pl.ds(c, 128), pl.ds(r, 128)] = tile.T.astype(target.dtype)


def spectrum(blocks, staged, twiddle):
    lanes = blocks[0].shape[0]
    for f, (re, im) in enumerate(outer_forward([block.astype(F32) for block in blocks])):
        c, s = twiddle[0, pl.ds(f, 1), :], twiddle[1, pl.ds(f, 1), :]
        staged[pl.ds(f * lanes, lanes), pl.ds(0, INNER)] = (re * c + im * s).astype(BF)
        staged[pl.ds(f * lanes, lanes), pl.ds(INNER, INNER)] = (im * c - re * s).astype(BF)


def both(data, matrix):
    return jnp.dot(data, matrix[0], preferred_element_type=F32) + jnp.dot(data, matrix[1], preferred_element_type=F32)


def kernel(
    act_hbm, weight, taps_hbm, blocks_hbm, gains_hbm, forward_hbm, inverse_hbm, twiddle_hbm,
    out,
    act, taps, blocks, gains, forward, inverse, twiddle,
    wbuf, kv, qs,
    a_z1, a_z2, a_zx, a_x1, a_x2, a_x3,
    b_z1, b_z2, b_zx, b_x1, b_x2, b_x3,
    q_z1, q_z2, q_zx, q_x1, q_x2, q_x3,
    taps_out, taps_in, taps_t, filt_in, staged, filt_spec, gain_t,
    gated, gated_t, gated_in, mixed, conv_out, conv_in, conv_home, conv_final,
    w_sems, in_sems, send_sems, recv_sems,
    *, depth, tp_count, ctx_count,
):
    place = Place(depth, tp_count, ctx_count)
    me, tp = place.ctx, place.tp
    tokens, width = gated.shape
    out_tokens = tokens // tp_count
    channels = tp_count * width
    tile = wbuf.shape[2]
    piece = width // SETS
    lanes = piece // ctx_count
    spots = ctx_count // SIDES
    part = lanes * spots
    side, spot = me // spots, me % spots
    crowd = SIDES * tp_count

    order = [step[1:] for step in SCHEDULE if step[0] == "mm"]
    tiles = []
    for own, step, c in order:
        base = place.owner(own, step) * width + c * part
        tiles.append([(which * channels + base + side * piece, part) for which in (1, 2) for side in range(SIDES)])
    for t in range(channels // tile):
        tiles.append([(t * tile, tile)])

    def fetch(t, act_on):
        at = 0
        for k, (column, size) in enumerate(tiles[t]):
            src = weight.at[:, pl.ds(pl.multiple_of(column, size), size)]
            act_on(pltpu.make_async_copy(src, wbuf.at[t, :, pl.ds(at, size)], w_sems.at[4 * t + k]))
            at += size

    barrier = pltpu.get_barrier_semaphore()

    def greet(device):
        pl.semaphore_signal(barrier, inc=1, device_id=device, device_id_type=pl.DeviceIdType.MESH)

    def across(away):
        return (me + away) % ctx_count

    other = (me + spots) % ctx_count
    half = spots // 2
    greet((me, place.owner(0, 2)))
    for away in (spots + half + 1, spots + half, spots + half - 1):
        greet((across(away), tp))
    for own in (0, 1):
        greet((other, place.owner(own, 2)))
    for step in (1, 3):
        greet((me, place.owner(0, step)))
    greet((me, place.owner(1, 2)))
    for away in range(1, ctx_count):
        if away not in (spots + half + 1, spots + half, spots + half - 1):
            greet((across(away), tp))
    for step in (1, 3):
        for own in (0, 1):
            greet((other, place.owner(own, step)))
    greet((other, place.owner(0, 0)))
    for step in (1, 3):
        greet((me, place.owner(1, step)))
    greet(place.far)

    pairs = ((act_hbm, act), (taps_hbm, taps), (blocks_hbm, blocks), (gains_hbm, gains),
             (forward_hbm, forward), (inverse_hbm, inverse), (twiddle_hbm, twiddle))
    inputs = [pltpu.make_async_copy(source, target, in_sems.at[k]) for k, (source, target) in enumerate(pairs)]
    inputs[0].start()
    fetch(0, lambda copy: copy.start())

    ahead = 4
    for t in range(1, ahead):
        fetch(t, lambda copy: copy.start())
    for copy in inputs[1:]:
        copy.start()

    def next_tile(t):
        fetch(t, lambda copy: copy.wait())
        if t + ahead < len(tiles):
            fetch(t + ahead, lambda copy: copy.start())

    inputs[0].wait()

    links = Links(send_sems, recv_sems)

    def over_crowd(src, dst):
        device = lambda peer: (peer // tp_count * spots + spot, peer % tp_count)
        return Swap(links, crowd, side * tp_count + tp, device, src, dst)

    def over_side(src, dst):
        return Swap(links, spots, spot, lambda peer: (side * spots + peer, tp), src, dst)

    def over_ctx(src, dst):
        return Swap(links, ctx_count, me, lambda peer: (peer, tp), src, dst)

    def span(index, size):
        return pl.ds(pl.multiple_of(index * size, size), size)

    tap_swap = over_crowd(
        lambda peer: taps_out.at[:, span(peer % tp_count * SIDES + peer // tp_count, piece)], lambda mine: taps_in.at[mine]
    )
    filt_swap = over_side(lambda peer: taps_t.at[:, span(peer, lanes)], lambda mine: filt_in.at[mine])
    gated_swap, conv_swap, home_swap = [], [], []
    for c in range(SETS):
        gated_swap.append(over_ctx(lambda peer, c=c: gated_t.at[c, span(peer, lanes)], lambda mine, c=c: gated_in.at[c, mine]))
        conv_swap.append(over_side(lambda peer, c=c: conv_out.at[c, peer], lambda mine, c=c: conv_in.at[c, span(mine, lanes)]))
        home_swap.append(over_crowd(lambda peer, c=c: conv_home.at[c, span(peer, out_tokens)], lambda mine, c=c: conv_final.at[c, mine]))

    def send_taps():
        inputs[1].wait()
        taps_out[...] = taps[...].astype(BF)
        tap_swap.start()

    def kv_part(c):
        def part(owner, which, half):
            rows = pl.ds(0, ROWS_Z) if which == 0 else pl.ds(ROWS_Z, tokens - ROWS_Z)
            return kv.at[owner, rows, pl.ds((2 * c + half) * piece, piece)]
        return part

    z_half, x_half = LANES_Z // 2, (channels - LANES_Z) // 2

    def q_part(owner, which, half):
        return qs.at[owner, :, pl.ds(half * z_half, z_half) if which == 0 else pl.ds(LANES_Z + half * x_half, x_half)]

    spreads = (
        Spread(place, links, kv_part(0), (a_z1, a_z2, a_zx, a_x1, a_x2, a_x3)),
        Spread(place, links, kv_part(1), (b_z1, b_z2, b_zx, b_x1, b_x2, b_x3)),
        Spread(place, links, q_part, (q_z1, q_z2, q_zx, q_x1, q_x2, q_x3)),
    )

    def multiply_kv(own, step, c):
        t = order.index((own, step, c))
        next_tile(t)
        block = jnp.dot(act[...], wbuf[t], preferred_element_type=F32)
        kv[place.owner(own, step), :, pl.ds(c * tile, tile)] = block.astype(BF)

    def multiply_q(t):
        next_tile(len(order) + t)
        block = jnp.dot(act[...], wbuf[len(order) + t], preferred_element_type=F32).astype(BF)
        qs[:, :, pl.ds(t * tile, tile)] = block.reshape(tp_count, out_tokens, tile)

    def mask():
        for copy in inputs[2:]:
            copy.wait()
        tap_swap.wait_recv()
        taps_in[side * tp_count + tp] = taps_out[:, span(tp * SIDES + side, piece)]
        for c in range(SETS):
            at = span((tp * SIDES + side) * SETS + c, part)
            depth_of = blocks[at].reshape(1, part)
            gain_t[c] = jnp.broadcast_to(gains[at].reshape(1, part), (part, part)).T
            for n in range(crowd * out_tokens // INNER):
                per = INNER // out_tokens
                block = taps_in[pl.ds(n * per, per), :, pl.ds(c * part, part)].reshape(INNER, part).astype(F32)
                index = n * INNER // tokens * spots + spot
                taps_t[c, :, pl.ds(n * INNER, INNER)] = jnp.where(index < depth_of, block, 0.0).T.astype(BF)
        filt_swap.start()

    rows = staged.shape[1] // 2

    fold = tokens // INNER

    def filter_spectrum():
        filt_swap.wait_recv()
        filt_in[spot] = taps_t[:, span(spot, lanes), :]
        for c in range(SETS):
            parts = []
            for a in range(OUTER):
                i, u = a // fold, a % fold
                parts.append(filt_in[i % spots, c, :, pl.ds((i // spots * fold + u) * INNER, INNER)])
            spectrum(parts, staged.at[c], twiddle)
            for n in range(2):
                at = pl.ds(n * rows, rows)
                filt_spec[c, at, :] = both(staged[c, at, :], forward)

    def finish(c):
        spreads[c].finish()
        if c < SETS:
            for which, at in ((0, pl.ds(0, ROWS_Z)), (1, pl.ds(ROWS_Z, tokens - ROWS_Z))):
                gated[at, pl.ds(c * piece, piece)] = spreads[c].total(which, 0) * spreads[c].total(which, 1)

    def gate(c):
        transposed(gated.at[:, pl.ds(c * piece, piece)], gated_t.at[c], tokens, piece)
        gated_swap[c].start()

    def convolve(c):
        gated_swap[c].wait_recv()
        gated_in[c, me] = gated_t[c, span(me, lanes), :]
        parts = [gated_in[c, a // fold, :, pl.ds(a % fold * INNER, INNER)] for a in range(OUTER)]
        spectrum(parts, staged.at[c], twiddle)
        for n in range(2):
            at = pl.ds(n * rows, rows)
            a = jnp.dot(staged[c, at, :], forward[0], preferred_element_type=F32)
            b = filt_spec[c, at, :]
            a_re, a_im, b_re, b_im = a[:, :INNER], a[:, INNER:], b[:, :INNER], b[:, INNER:]
            prod = jnp.concatenate([a_re * b_re - a_im * b_im, a_re * b_im + a_im * b_re], axis=1)
            mixed[at, :] = jnp.dot(prod.astype(BF), inverse[0], preferred_element_type=F32)
        data = []
        for f in range(OUTER):
            cos, sin = twiddle[0, pl.ds(f, 1), :], twiddle[1, pl.ds(f, 1), :]
            row = pl.ds(f * lanes, lanes)
            re, im = mixed[row, pl.ds(0, INNER)], mixed[row, pl.ds(INNER, INNER)]
            data.append((re * cos - im * sin, re * sin + im * cos))
        gain = gain_t[c, span(spot, lanes), :]
        for a, block in enumerate(outer_inverse(data)):
            i, u = a // fold, a % fold
            at = pl.ds((i // spots * fold + u) * INNER, INNER)
            conv_out[c, i % spots, :, at] = (block + gain * parts[a].astype(F32)).astype(BF)
        conv_swap[c].start()

    def home(c):
        conv_swap[c].wait_recv()
        conv_in[c, span(spot, lanes), :] = conv_out[c, spot]
        transposed(conv_in.at[c], conv_home.at[c], part, SIDES * tokens)
        home_swap[c].start()

    def finale():
        query = jnp.concatenate([spreads[SETS].total(which, half) for which in (0, 1) for half in (0, 1)], axis=1)
        for c in [step[1] for step in SCHEDULE if step[0] == "home"]:
            home_swap[c].wait_recv()
            conv_final[c, side * tp_count + tp] = conv_home[c, span(side * tp_count + tp, out_tokens), :]
            for peer in range(crowd):
                first = ((peer % tp_count * SIDES + peer // tp_count) * SETS + c) * part
                at = slice(first, first + part)
                out[:, at] = (query[:, at] * conv_final[c, peer].astype(F32)).astype(BF)

    steps = {
        "bar": lambda: pl.semaphore_wait(barrier, 2 * tp_count + ctx_count - 3),
        "mm": multiply_kv,
        "mq": multiply_q,
        "tap": send_taps,
        "mask": mask,
        "filt": filter_spectrum,
        "z1": lambda c, own: spreads[c].start_z1(own),
        "x1": lambda c, step: spreads[c].start_x1(step),
        "z2f": lambda c, own, way: spreads[c].start_z2_free(own, way),
        "pz1": lambda c, own, way: spreads[c].pass_z1(own, way),
        "tx1": lambda c, step: spreads[c].take_x1(step),
        "x2": lambda c: spreads[c].start_x2(),
        "x3f": lambda c, way: spreads[c].start_x3_free(way),
        "px2": lambda c, way: spreads[c].pass_x2(way),
        "zx": lambda c, half: spreads[c].start_zx(half),
        "fin": finish,
        "gate": gate,
        "conv": convolve,
        "home": home,
        "out": finale,
        "drain": links.drain,
    }
    for step in SCHEDULE:
        steps[step[0]](*step[1:])

    links.drain(len(links.started))


def on_device(activations, proj_weight, filter_taps, filter_blocks, skip_gain):
    tokens, depth_here = activations.shape
    channels, out_tokens = filter_taps.shape
    tp_count, ctx_count = lax.axis_size("tp"), lax.axis_size("ctx")
    depth = 4
    width = channels // tp_count
    forward, inverse, twiddle = tables()

    def buffers(z_rows, z_lanes, x_rows, x_lanes):
        return [
            pltpu.VMEM((2, 2, z_rows, z_lanes), BF),
            pltpu.VMEM((2, 2, 2, z_rows, z_lanes), BF),
            pltpu.VMEM((2, z_rows, z_lanes), BF),
            pltpu.VMEM((4, 2, x_rows, x_lanes), BF),
            pltpu.VMEM((2, x_rows, x_lanes), BF),
            pltpu.VMEM((2, 2, x_rows, x_lanes), BF),
        ]

    tile = width
    n_tiles = 3 * channels // tile
    n_copies = (SETS + 1) * 28 + (1 + SETS) * (2 * tp_count + ctx_count // SIDES - 2) + SETS * (ctx_count - 1)
    piece = width // SETS
    lanes = piece // ctx_count
    spots = ctx_count // SIDES
    part = lanes * spots
    crowd = SIDES * tp_count
    spec_rows = OUTER * lanes
    scratch = (
        [
            pltpu.VMEM((tokens, depth_here), BF),
            pltpu.VMEM((out_tokens, channels), F32),
            pltpu.VMEM((channels,), jnp.int32),
            pltpu.VMEM((channels,), F32),
            pltpu.VMEM(forward.shape, BF),
            pltpu.VMEM(inverse.shape, BF),
            pltpu.VMEM(twiddle.shape, F32),
            pltpu.VMEM((n_tiles, depth_here, tile), BF),
            pltpu.VMEM((tp_count, tokens, 2 * width), BF),
            pltpu.VMEM((tp_count, out_tokens, channels), BF),
        ]
        + buffers(ROWS_Z, piece, tokens - ROWS_Z, piece)
        + buffers(ROWS_Z, piece, tokens - ROWS_Z, piece)
        + buffers(out_tokens, LANES_Z // 2, out_tokens, (channels - LANES_Z) // 2)
        + [
            pltpu.VMEM((out_tokens, channels), BF),
            pltpu.VMEM((crowd, out_tokens, piece), BF),
            pltpu.VMEM((SETS, part, SIDES * tokens), BF),
            pltpu.VMEM((spots, SETS, lanes, SIDES * tokens), BF),
            pltpu.VMEM((SETS, spec_rows, 2 * INNER), BF),
            pltpu.VMEM((SETS, spec_rows, 2 * INNER), F32),
            pltpu.VMEM((SETS, part, part), F32),
            pltpu.VMEM((tokens, width), F32),
            pltpu.VMEM((SETS, piece, tokens), BF),
            pltpu.VMEM((SETS, ctx_count, lanes, tokens), BF),
            pltpu.VMEM((spec_rows, 2 * INNER), F32),
            pltpu.VMEM((SETS, spots, lanes, SIDES * tokens), BF),
            pltpu.VMEM((SETS, part, SIDES * tokens), BF),
            pltpu.VMEM((SETS, SIDES * tokens, part), BF),
            pltpu.VMEM((SETS, crowd, out_tokens, part), BF),
            pltpu.SemaphoreType.DMA((4 * n_tiles,)),
            pltpu.SemaphoreType.DMA((7,)),
            pltpu.SemaphoreType.DMA((n_copies,)),
            pltpu.SemaphoreType.DMA((n_copies,)),
        ]
    )
    vmem = pl.BlockSpec(memory_space=pltpu.VMEM)
    out = pl.pallas_call(
        functools.partial(kernel, depth=depth, tp_count=tp_count, ctx_count=ctx_count),
        out_shape=pltpu.VMEM((out_tokens, channels), BF),
        in_specs=[pl.BlockSpec(memory_space=pl.ANY)] * 8,
        out_specs=vmem,
        scratch_shapes=scratch,
        compiler_params=pltpu.CompilerParams(collective_id=0, has_side_effects=True, vmem_limit_bytes=60 * 2**20),
        name="hyena",
    )(
        activations,
        proj_weight,
        filter_taps.T,
        filter_blocks,
        skip_gain,
        jnp.asarray(forward),
        jnp.asarray(inverse),
        jnp.asarray(twiddle),
    )
    return out.T


def solution(mesh):
    placed = (P("ctx", "tp"), P("tp", None), P(None, ("ctx", "tp")), P(), P())
    return jax.shard_map(
        on_device, mesh=mesh, in_specs=placed, out_specs=P(None, ("ctx", "tp")), check_vma=False
    )
```
